256 devices in a mesh: frame: 16 (over z_lo, y, core), mp: 16 (over z_hi, x).
Axes of the slice: x: 4, y: 4, z: 8 (z_hi: 4, z_lo: 2; z = z_hi * 2 + z_lo), core: 2. Of those that a mesh axis runs over, the one named last changes fastest.
Arguments:
- tokens: bfloat16 [128, 2, 32, 3072], P('mp', None, 'frame'), may hold values from -6 to 6
- cotangent: bfloat16 [128, 2, 32, 3072], P('mp', None, 'frame'), may hold values from -8 to 8
- mod_shift: float32 [2, 32, 3072], P(None, 'frame'), may hold values from -3 to 3
- mod_scale: float32 [2, 32, 3072], P(None, 'frame'), may hold values from -0.5 to 5
- mod_gate: float32 [2, 32, 3072], P(None, 'frame'), may hold values from -4 to 4
- attn_weights: bfloat16 [3072, 4, 4096], P(None, None, 'mp'), may hold values from -1 to 1
Outputs:
- mixed: bfloat16 [128, 2, 32, 3072], P('mp', None, 'frame')
- grad_tokens: bfloat16 [128, 2, 32, 3072], P('mp', None, 'frame')
- weight_grads: float32 [3072, 4, 4096], P('frame', None, 'mp')
The draws below stay inside these ranges and needn't reach their ends.
All inputs are finite; a program needn't handle non-finite values.
Results may differ from the reference program's by a relative error of at most 0.023.
Values may be sent and summed in bfloat16 or wider, within the bound.
A program may use at most 128 MiB of HBM per device.

```python
import jax
import jax.numpy as jnp
from jax import lax

D = 3072
HD = 128
PATCH = 128
CLIPS = 2
HEADS = 32
INNER = 4096
FRAMES = 32


def draw_mod_scale(key, part):
    key = jax.random.fold_in(key, 11)
    key_entry = jax.random.fold_in(key, 1)
    return jax.random.uniform(key_entry, (CLIPS, FRAMES, D), jnp.float32, -0.5, 1.0)


def draw_attn_weights(key, part):
    key = jax.random.fold_in(key, 23)
    sub_keys = jax.random.split(key, 4)
    shape = (D, INNER)
    noise = [jax.random.truncated_normal(sub_key, -4.0, 4.0, shape, jnp.float32) for sub_key in sub_keys]
    model_scale = D ** (-0.5)
    w_query = noise[0] * model_scale
    w_key = (0.6 * noise[0] + 0.8 * noise[1]) * model_scale
    w_value = noise[2] * model_scale
    w_out = noise[3] * INNER ** (-0.5)
    return jnp.stack([w_query, w_key, w_value, w_out], axis=1).astype(jnp.bfloat16)


def raised(values, own_key, source, target, parts, factor):
    owner, partner = [(jnp.arange(values.shape[dim]) // (values.shape[dim] // parts)).reshape([-1 if axis == dim else 1 for axis in range(values.ndim)]) for dim in (source, target)]
    chosen = jax.random.permutation(own_key, parts)[partner]
    strong = (owner == chosen) | (owner == (partner + parts // 2) % parts)
    return jnp.where(strong, factor * values, values)


def block_scale(rng, extent, cuts, low, top_value):
    def one(dim, blocks):
        heights = jax.random.uniform(jax.random.fold_in(jax.random.fold_in(rng, 6), dim), (blocks,), jnp.float32, low / len(cuts), top_value / len(cuts))
        return jnp.repeat(jnp.exp(heights), extent[dim] // blocks).reshape((-1,) + (1,) * (len(extent) - dim - 1))

    level = one(*cuts[0])
    for cut in cuts[1:]:
        level = level * one(*cut)
    return level


def centred(stream_key, extent, scale, limit, shards=(), dtype=jnp.bfloat16):
    level = block_scale(stream_key, extent, shards, -0.22, 0.18) if shards else 1.0
    result = jax.random.normal(stream_key, extent, jnp.float32) * scale * level
    return jnp.minimum(jnp.maximum(result, -limit), limit).astype(dtype)


def heavy_noise(rng, extent, deviation, limit, cuts, heavy, held_as=jnp.bfloat16):
    result = deviation * jax.random.normal(rng, extent, jnp.float32)
    if cuts:
        result = result * block_scale(rng, extent, cuts, -0.22, 0.18)
    return jnp.clip(raised(result, jax.random.fold_in(rng, 3), *heavy), -limit, limit).astype(held_as)


def setup_inputs(seed: int = 0) -> dict:
    streams_of = jax.random.split(jax.random.key(seed), 7)
    tokens = centred(streams_of[0], (PATCH, CLIPS, FRAMES, D), 1.0, 6.0, ((0, 16), (2, 16)))
    cotangent = heavy_noise(streams_of[1], (PATCH, CLIPS, FRAMES, D), 1.0, 8.0, ((0, 16), (2, 16)), (2, 3, 16, 2.0))
    mod_shift = centred(streams_of[2], (CLIPS, FRAMES, D), 0.5, 3.0, ((1, 16),), jnp.float32)
    mod_scale = draw_mod_scale(jax.random.fold_in(streams_of[6], 71), 0)
    mod_gate = centred(streams_of[4], (CLIPS, FRAMES, D), 1.0, 4.0, ((1, 16),), jnp.float32)
    attn_weights = draw_attn_weights(jax.random.fold_in(streams_of[6], 71), 0)
    return {"tokens": tokens, "cotangent": cotangent, "mod_shift": mod_shift, "mod_scale": mod_scale, "mod_gate": mod_gate, "attn_weights": attn_weights}


EPSILON = 1e-06

def modulate(tokens, mod_shift, mod_scale):
    values = tokens.astype(jnp.float32)
    inverse_rms = lax.rsqrt(lax.optimization_barrier(jnp.mean(values * values, axis=-1, keepdims=True)) + EPSILON)
    unit_rows = values * inverse_rms
    normalized_rows = (unit_rows * (1.0 + mod_scale) + mod_shift).astype(jnp.bfloat16)
    return (normalized_rows, unit_rows, inverse_rms)

def reference(tokens, cotangent, mod_shift, mod_scale, mod_gate, attn_weights):
    factor = HD ** (-0.5)
    row_total = PATCH * CLIPS * FRAMES
    normalized_rows, unit_rows, inverse_rms = modulate(tokens, mod_shift, mod_scale)
    flat_normed = normalized_rows.reshape(row_total, D)

    def project(slot_index):
        product = jnp.dot(flat_normed, attn_weights[:, slot_index, :], preferred_element_type=jnp.float32)
        return product.astype(jnp.bfloat16).reshape(PATCH, CLIPS, FRAMES, HEADS, HD)
    query = project(0)
    key_rows = project(1)
    value_rows = project(2)
    scores = jnp.einsum('pbfne,pbgne->pbnfg', query.astype(jnp.float32), key_rows.astype(jnp.float32)) * factor
    attention = jax.nn.softmax(scores, axis=-1)
    attention_low = attention.astype(jnp.bfloat16)
    attended = jnp.einsum('pbnfg,pbgne->pbfne', attention_low.astype(jnp.float32), value_rows.astype(jnp.float32)).astype(jnp.bfloat16)
    attended_flat = attended.reshape(row_total, INNER)
    w_out = attn_weights[:, 3, :]
    branch = jnp.dot(attended_flat, w_out.T, preferred_element_type=jnp.float32).reshape(PATCH, CLIPS, FRAMES, D)
    mixed = (tokens.astype(jnp.float32) + mod_gate * branch).astype(jnp.bfloat16)
    scaled_cot = (cotangent.astype(jnp.float32) * mod_gate).astype(jnp.bfloat16)
    scaled_flat = scaled_cot.reshape(row_total, D)
    grad_attended = jnp.dot(scaled_flat, w_out, preferred_element_type=jnp.float32).astype(jnp.bfloat16)
    grad_attended = grad_attended.reshape(PATCH, CLIPS, FRAMES, HEADS, HD)
    grad_value = jnp.einsum('pbnfg,pbfne->pbgne', attention_low.astype(jnp.float32), grad_attended.astype(jnp.float32)).astype(jnp.bfloat16)
    grad_probs = jnp.einsum('pbfne,pbgne->pbnfg', grad_attended.astype(jnp.float32), value_rows.astype(jnp.float32))
    grad_scores = (attention * (grad_probs - lax.optimization_barrier(jnp.sum(grad_probs * attention, axis=-1, keepdims=True))) * factor).astype(jnp.bfloat16)
    grad_query = jnp.einsum('pbnfg,pbgne->pbfne', grad_scores.astype(jnp.float32), key_rows.astype(jnp.float32)).astype(jnp.bfloat16)
    grad_key = jnp.einsum('pbnfg,pbfne->pbgne', grad_scores.astype(jnp.float32), query.astype(jnp.float32)).astype(jnp.bfloat16)
    flat_query = grad_query.reshape(row_total, INNER)
    flat_key = grad_key.reshape(row_total, INNER)
    flat_value = grad_value.reshape(row_total, INNER)
    grad_normed = jnp.dot(flat_query, attn_weights[:, 0, :].T, preferred_element_type=jnp.float32)
    grad_normed = grad_normed + jnp.dot(flat_key, attn_weights[:, 1, :].T, preferred_element_type=jnp.float32)
    grad_normed = grad_normed + jnp.dot(flat_value, attn_weights[:, 2, :].T, preferred_element_type=jnp.float32)
    grad_unit = grad_normed.reshape(PATCH, CLIPS, FRAMES, D) * (1.0 + mod_scale)
    correction = lax.optimization_barrier(jnp.mean(grad_unit * unit_rows, axis=-1, keepdims=True))
    grad_tokens = (cotangent.astype(jnp.float32) + inverse_rms * (grad_unit - unit_rows * correction)).astype(jnp.bfloat16)
    weight_grads = jnp.stack([jnp.dot(flat_normed.T, flat_query, preferred_element_type=jnp.float32), jnp.dot(flat_normed.T, flat_key, preferred_element_type=jnp.float32), jnp.dot(flat_normed.T, flat_value, preferred_element_type=jnp.float32), jnp.dot(scaled_flat.T, attended_flat, preferred_element_type=jnp.float32)], axis=1)
    return (mixed, grad_tokens, weight_grads)
```

```python
import jax
import jax.numpy as jnp
from jax import lax
from jax.experimental import pallas as pl
from jax.experimental.pallas import tpu as pltpu
from jax.sharding import PartitionSpec as P

HD = 128
D = 3072
EPSILON = 1e-06
MESH = pl.DeviceIdType.MESH
BF16 = jnp.bfloat16
F32 = jnp.float32
MIB = 1024 * 1024


def dot(a, b, dims=((1,), (0,))):
    return lax.dot_general(a, b, (dims, ((), ())), preferred_element_type=F32)


NT = ((1,), (1,))
TN = ((0,), (0,))


class Ring:
    def __init__(self, index, device, stride):
        self.index, self.device, self.stride = index, device, stride

    def at(self, step):
        return lax.rem(self.index + (step + 4), 4)

    def to(self, step):
        return self.device(self.at(step))


class Links:
    def __init__(self, send_sems, recv_sems):
        self.send_sems, self.recv_sems = send_sems, recv_sems
        self.copies = []

    def copy(self, source, target, device):
        number = len(self.copies)
        made = pltpu.make_async_remote_copy(
            src_ref=source,
            dst_ref=target,
            send_sem=self.send_sems.at[number],
            recv_sem=self.recv_sems.at[number],
            device_id=device,
            device_id_type=MESH,
        )
        self.copies.append(made)
        return made

    def drain(self):
        for made in self.copies:
            made.wait_send()


def block_rows(first, second, one, two, half):
    block = first.at(one) * first.stride + second.at(two) * second.stride
    start = block * 32 + (0 if half is None else 16 * half)
    size = 32 if half is None else 16
    return pl.ds(pl.multiple_of(start, size), size)


def gather_events(links, buffer, columns, first, second):
    def message(ring, step, one, two, half=None):
        part = buffer.at[block_rows(first, second, one, two, half), columns]
        return links.copy(part, part, ring.to(step))

    ahead, back = message(first, 1, 0, 0), message(first, -1, 0, 0)
    ahead_far, back_far = message(first, 1, -1, 0, 0), message(first, -1, 1, 0, 1)
    near, far = {}, {}
    for one in (0, -1, 1, 2):
        near[one] = message(second, 1, one, 0), message(second, -1, one, 0)
        far[one] = message(second, 1, one, -1, 0), message(second, -1, one, 1, 1)

    def begin():
        for made in (ahead, back) + near[0]:
            made.start()

    def from_behind():
        ahead.wait_recv()
        for made in (ahead_far,) + near[-1]:
            made.start()

    def from_ahead():
        back.wait_recv()
        for made in (back_far,) + near[1]:
            made.start()

    def from_across():
        ahead_far.wait_recv()
        back_far.wait_recv()
        for made in near[2]:
            made.start()

    def onward(one):
        def event():
            for arrived, following in zip(near[one], far[one]):
                arrived.wait_recv()
                following.start()

        return event

    def end():
        for pair in far.values():
            for made in pair:
                made.wait_recv()

    return [begin, from_behind, from_ahead, onward(0), from_across, onward(-1), onward(1), onward(2), end]


def add_to(target, *others):
    total = target[...].astype(F32)
    for other in others:
        total = total + other[...].astype(F32)
    target[...] = total.astype(target.dtype)


class RingSum:
    def __init__(self, links, ring, piece, first, second):
        self.piece, self.first, self.second = piece, first, second
        ahead, back = ring.to(1), ring.to(-1)
        self.far = (
            links.copy(piece(2, 0), first(0), ahead),
            links.copy(piece(2, 1), first(1), back),
        )
        self.own = (
            links.copy(piece(1, 1), second(0, 1), ahead),
            links.copy(piece(-1, 0), second(1, 0), back),
        )
        self.summed = (
            links.copy(piece(1, 0), second(0, 0), ahead),
            links.copy(piece(-1, 1), second(1, 1), back),
        )

    def begin(self):
        for made in self.far + self.own:
            made.start()

    def onward(self):
        for side, target in enumerate((self.piece(1, 0), self.piece(-1, 1))):
            self.far[side].wait_recv()
            add_to(target, self.first(side))
            self.summed[side].start()

    def end(self):
        for made in self.own + self.summed:
            made.wait_recv()
        for half in range(2):
            add_to(self.piece(0, half), self.second(0, half), self.second(1, half))


def scatter_events(links, buffer, columns, first, second, land1, land2):
    def over_first(slot, two):
        return RingSum(
            links,
            first,
            lambda one, half: buffer.at[block_rows(first, second, one, two, half), columns],
            lambda side: land1.at[slot, side, :, columns],
            lambda side, half: land2.at[slot, side, 16 * half : 16 * half + 16, columns],
        )

    rows = [over_first(slot, two) for slot, two in enumerate((2, -1, 1, 0))]
    column = RingSum(
        links,
        second,
        lambda two, half: buffer.at[block_rows(first, second, 0, two, half), columns],
        lambda side: land1.at[4, side, :, columns],
        lambda side, half: land2.at[4, side, 16 * half : 16 * half + 16, columns],
    )

    def begin():
        for row in rows:
            row.begin()

    def onward(row):
        return row.onward

    def end_rows():
        for row in rows:
            row.end()

    return [begin] + [row.onward for row in rows] + [end_rows, column.begin, column.onward, column.end]


def softmax_rows(scores):
    shifted = jnp.exp(scores - jnp.max(scores, axis=-1, keepdims=True))
    return shifted / jnp.sum(shifted, axis=-1, keepdims=True)


def same_block():
    rows = lax.broadcasted_iota(jnp.int32, (HD, HD), 0)
    columns = lax.broadcasted_iota(jnp.int32, (HD, HD), 1)
    return (rows >> 5) == (columns >> 5)


def kernel(
    x0, w_hbm, out, dw,
    xall, w, qkv, grad_att, dall, turned, probs, branch, grad, dpart,
    land1b, land2b, land1g, land2g, land_core, land1y, land2y, land_z, flipped, core_out, core_in,
    send_sems, recv_sems, local_sems,
):
    f, m = lax.axis_index("frame"), lax.axis_index("mp")
    x, z = lax.rem(m, 4), lax.div(m, 4)
    core, y, zl = lax.rem(f, 2), lax.rem(lax.div(f, 2), 4), lax.div(f, 8)
    other = 1 - core
    ring_x = Ring(x, lambda to: (f, z * 4 + to), 1)
    ring_z = Ring(z, lambda to: (f, to * 4 + x), 4)
    ring_y = Ring(y, lambda to: (zl * 8 + to * 2 + core, m), 0)
    z_partner = ((1 - zl) * 8 + y * 2 + core, m)
    core_partner = (zl * 8 + y * 2 + other, m)
    links = Links(send_sems, recv_sems)

    own_rows = pl.ds(pl.multiple_of(m * 32, 32), 32)
    take = pltpu.make_async_copy(x0, xall.at[own_rows, :], local_sems.at[0])
    take.start()
    weigh = pltpu.make_async_copy(w_hbm, w, local_sems.at[1])
    weigh.start()
    barrier = pltpu.get_barrier_semaphore()
    for ring in (ring_x, ring_z, ring_y):
        for step in (1, -1):
            pl.semaphore_signal(barrier, inc=1, device_id=ring.to(step), device_id_type=MESH)
    for partner in (z_partner, core_partner):
        pl.semaphore_signal(barrier, inc=1, device_id=partner, device_id_type=MESH)
    pl.semaphore_wait(barrier, 8)
    take.wait()

    normed = gather_events(links, xall, slice(0, D), ring_z, ring_x)
    scaled = gather_events(links, xall, slice(D, 2 * D), ring_z, ring_x)
    sum_branch = scatter_events(links, branch, slice(0, D), ring_x, ring_z, land1b, land2b)
    sum_grad = scatter_events(links, grad, slice(0, D), ring_x, ring_z, land1g, land2g)

    def chip_columns(y_to, zl_to):
        return pl.ds(pl.multiple_of(zl_to * 1536 + y_to * 384, 128), 384)

    mine = pl.multiple_of(core * 512, 512)
    theirs = pl.multiple_of(other * 512, 512)
    chunks = [(step, side) for step in (2, 1, -1, 0) for side in (1, 0)]
    core_copies = {}
    for step, side in chunks:
        columns = chip_columns(ring_y.at(step), lax.rem(zl + side, 2))
        core_copies[step, side] = links.copy(
            dpart.at[pl.ds(theirs, 512), columns], land_core.at[:, columns], core_partner
        )

    def over_y(side):
        zl_to = lax.rem(zl + side, 2)
        return RingSum(
            links,
            ring_y,
            lambda step, half: dpart.at[
                pl.ds(pl.multiple_of(mine + 256 * half, 256), 256), chip_columns(ring_y.at(step), zl_to)
            ],
            lambda go: land1y.at[side, go],
            lambda go, half: land2y.at[side, go, 256 * half : 256 * half + 256],
        )

    y_sums = [over_y(0), over_y(1)]
    z_copy = links.copy(
        dpart.at[pl.ds(mine, 512), chip_columns(y, 1 - zl)], land_z, z_partner
    )
    core_copy = links.copy(core_out, core_in, core_partner)

    def project(slot):
        qkv[:, 256 * slot : 256 * slot + 256] = dot(
            xall[:, :D], w[:, 256 * slot : 256 * slot + 256]
        ).astype(BF16)

    def attend():
        mask = same_block()

        @pl.loop(0, 4)
        def _(group):
            rows = pl.ds(pl.multiple_of(group * HD, HD), HD)
            for head in range(2):
                query = qkv[rows, head * HD : head * HD + HD]
                key = qkv[rows, 256 + head * HD : 256 + head * HD + HD]
                value = qkv[rows, 512 + head * HD : 512 + head * HD + HD]
                scores = dot(query, key, NT) * (HD ** -0.5)
                attention = softmax_rows(jnp.where(mask, scores, -1e30))
                probs[group * 2 + head] = attention
                dall[rows, 768 + head * HD : 768 + head * HD + HD] = dot(
                    attention.astype(BF16), value
                ).astype(BF16)

    def branch_part(step):
        rows = pl.ds(pl.multiple_of(step * 512, 512), 512)
        branch[:, rows] = dot(dall[:, 768:], w[rows, 768:], NT).astype(BF16)

    def all_branch():
        pl.loop(0, 6)(branch_part)

    def back_project():
        grad_att[...] = dot(xall[:, D:], w[:, 768:]).astype(BF16)

    def attend_back():
        @pl.loop(0, 4)
        def _(group):
            rows = pl.ds(pl.multiple_of(group * HD, HD), HD)
            for head in range(2):
                low = slice(head * HD, head * HD + HD)
                query = qkv[rows, head * HD : head * HD + HD]
                key = qkv[rows, 256 + head * HD : 256 + head * HD + HD]
                value = qkv[rows, 512 + head * HD : 512 + head * HD + HD]
                incoming = grad_att[rows, low]
                attention = probs[group * 2 + head]
                grad_probs = dot(incoming, value, NT)
                inner = jnp.sum(grad_probs * attention, axis=-1, keepdims=True)
                grad_scores = (attention * (grad_probs - inner) * (HD ** -0.5)).astype(BF16)
                dall[rows, head * HD : head * HD + HD] = dot(grad_scores, key).astype(BF16)
                dall[rows, 256 + head * HD : 256 + head * HD + HD] = dot(
                    grad_scores, query, TN
                ).astype(BF16)
                dall[rows, 512 + head * HD : 512 + head * HD + HD] = dot(
                    attention.astype(BF16), incoming, TN
                ).astype(BF16)

    def grad_part(step):
        rows = pl.ds(pl.multiple_of(step * 512, 512), 512)
        grad[:, rows] = dot(dall[:, :768], w[rows, :768], NT).astype(BF16)

    def all_grad():
        pl.loop(0, 6)(grad_part)

    def turn():
        for part in range(8):
            turned[part * HD : part * HD + HD, :] = dall[:, part * HD : part * HD + HD].T

    def weight_chunk(step, side):
        def event():
            zl_to = lax.rem(zl + side, 2)
            columns = chip_columns(ring_y.at(step), zl_to)
            gated = pl.ds(pl.multiple_of(D + zl_to * 1536 + ring_y.at(step) * 384, 128), 384)
            dpart[:768, columns] = dot(turned[:768, :], xall[:, columns]).astype(BF16)
            dpart[768:, columns] = dot(turned[768:, :], xall[:, gated]).astype(BF16)
            core_copies[step, side].start()

        return event

    def core_sum(step, side):
        def event():
            columns = chip_columns(ring_y.at(step), lax.rem(zl + side, 2))
            core_copies[step, side].wait_recv()
            add_to(dpart.at[pl.ds(mine, 512), columns], land_core.at[:, columns])

        return event

    def z_end():
        z_copy.wait_recv()
        columns = chip_columns(y, zl)
        total = dpart[pl.ds(mine, 512), columns].astype(F32) + land_z[...].astype(F32)
        flipped[...] = total.T
        core_out[...] = flipped[pl.ds(pl.multiple_of(other * 192, 192), 192), :].astype(BF16)
        core_copy.start()
        dw[:, pl.ds(mine, 512)] = flipped[pl.ds(pl.multiple_of(core * 192, 192), 192), :]

    def core_end():
        core_copy.wait_recv()
        dw[:, pl.ds(theirs, 512)] = core_in[...].astype(F32)

    n, s, b, g = normed, scaled, sum_branch, sum_grad
    plan = [
        *n[:5], s[0], *n[5:8], s[1], s[2], n[8],
        weigh.wait,
        lambda: project(0), s[3], lambda: project(1), s[4], lambda: project(2), s[5],
        attend, s[6], all_branch, s[7],
        b[0],
        s[8],
        back_project, b[1], attend_back, b[2], all_grad, g[0], b[3], b[4],
        turn,
        *[weight_chunk(*chunk) for chunk in chunks[:4]],
        b[5], b[6],
        *[core_sum(*chunk) for chunk in chunks[:2]],
        *[weight_chunk(*chunk) for chunk in chunks[4:]],
        g[1], g[2],
        *[core_sum(*chunk) for chunk in chunks[2:6]],
        y_sums[1].begin, y_sums[0].begin,
        b[7], g[3], g[4],
        *[core_sum(*chunk) for chunk in chunks[6:]],
        b[8],
        y_sums[1].onward, y_sums[0].onward,
        g[5], g[6],
        y_sums[1].end, z_copy.start,
        g[7],
        y_sums[0].end,
        z_end,
        g[8],
        core_end,
    ]
    for event in plan:
        event()
    out[:, :D] = branch[own_rows, :]
    out[:, D:] = grad[own_rows, :]
    links.drain()


def exchange_and_compute(x0, weights):
    copies = 160
    return pl.pallas_call(
        kernel,
        out_shape=(
            jax.ShapeDtypeStruct((32, 2 * D), BF16),
            jax.ShapeDtypeStruct((192, 1024), F32),
        ),
        in_specs=[pl.BlockSpec(memory_space=pl.ANY)] * 2,
        out_specs=[pl.BlockSpec(memory_space=pltpu.VMEM)] * 2,
        scratch_shapes=[
            pltpu.VMEM((512, 2 * D), BF16),
            pltpu.VMEM((D, 1024), BF16),
            pltpu.VMEM((512, 768), BF16),
            pltpu.VMEM((512, 256), BF16),
            pltpu.VMEM((512, 1024), BF16),
            pltpu.VMEM((1024, 512), BF16),
            pltpu.VMEM((8, HD, HD), F32),
            pltpu.VMEM((512, D), BF16),
            pltpu.VMEM((512, D), BF16),
            pltpu.VMEM((1024, D), BF16),
            pltpu.VMEM((5, 2, 16, D), BF16),
            pltpu.VMEM((5, 2, 32, D), BF16),
            pltpu.VMEM((5, 2, 16, D), BF16),
            pltpu.VMEM((5, 2, 32, D), BF16),
            pltpu.VMEM((512, D), BF16),
            pltpu.VMEM((2, 2, 256, 384), BF16),
            pltpu.VMEM((2, 2, 512, 384), BF16),
            pltpu.VMEM((512, 384), BF16),
            pltpu.VMEM((384, 512), F32),
            pltpu.VMEM((192, 512), BF16),
            pltpu.VMEM((192, 512), BF16),
            pltpu.SemaphoreType.DMA((copies,)),
            pltpu.SemaphoreType.DMA((copies,)),
            pltpu.SemaphoreType.DMA((2,)),
        ],
        compiler_params=pltpu.CompilerParams(
            collective_id=0, has_side_effects=True, vmem_limit_bytes=60 * MIB
        ),
    )(x0, weights)


def on_device(tokens, cotangent, mod_shift, mod_scale, mod_gate, attn_weights):
    values = tokens.astype(F32)
    inverse_rms = lax.rsqrt(jnp.mean(values * values, axis=-1, keepdims=True) + EPSILON)
    unit = values * inverse_rms
    normed = (unit * (1.0 + mod_scale) + mod_shift).astype(BF16)
    scaled = (cotangent.astype(F32) * mod_gate).astype(BF16)
    rows = jnp.concatenate([normed, scaled], axis=-1).reshape(16, 2, 2 * D)
    rows = lax.all_to_all(rows, "frame", split_axis=0, concat_axis=0, tiled=True)
    sums, weight_grads = exchange_and_compute(
        rows.reshape(32, 2 * D), attn_weights.reshape(D, 1024)
    )
    sums = lax.all_to_all(
        sums.reshape(16, 2, 2 * D), "frame", split_axis=0, concat_axis=0, tiled=True
    ).reshape(8, 2, 2, 2 * D)
    branch, grad_normed = sums[..., :D].astype(F32), sums[..., D:].astype(F32)
    mixed = (values + mod_gate * branch).astype(BF16)
    grad_unit = grad_normed * (1.0 + mod_scale)
    correction = jnp.mean(grad_unit * unit, axis=-1, keepdims=True)
    grad_tokens = (
        cotangent.astype(F32) + inverse_rms * (grad_unit - unit * correction)
    ).astype(BF16)
    return mixed, grad_tokens, weight_grads.reshape(192, 4, 256)


def solution(mesh):
    placed = (
        P("mp", None, "frame", None),
        P("mp", None, "frame", None),
        P(None, "frame", None),
        P(None, "frame", None),
        P(None, "frame", None),
        P(None, None, "mp"),
    )
    return jax.shard_map(
        on_device,
        mesh=mesh,
        in_specs=placed,
        out_specs=(
            P("mp", None, "frame", None),
            P("mp", None, "frame", None),
            P("frame", None, "mp"),
        ),
        check_vma=False,
    )
```

```python
import jax
import jax.numpy as jnp
from jax import lax
from jax.experimental import pallas as pl
from jax.experimental.pallas import tpu as pltpu
from jax.sharding import PartitionSpec as P

HD = 128
D = 3072
EPSILON = 1e-06
MESH = pl.DeviceIdType.MESH
BF16 = jnp.bfloat16
F32 = jnp.float32
MIB = 1024 * 1024
SPLIT = 2432


def dot(a, b, dims=((1,), (0,))):
    return lax.dot_general(a, b, (dims, ((), ())), preferred_element_type=F32)


NT = ((1,), (1,))
TN = ((0,), (0,))


class Ring:
    def __init__(self, index, device, stride):
        self.index, self.device, self.stride = index, device, stride

    def at(self, step):
        return lax.rem(self.index + (step + 4), 4)

    def to(self, step):
        return self.device(self.at(step))


class Links:
    def __init__(self, send_sems, recv_sems):
        self.send_sems, self.recv_sems = send_sems, recv_sems
        self.copies = []

    def copy(self, source, target, device):
        number = len(self.copies)
        made = pltpu.make_async_remote_copy(
            src_ref=source,
            dst_ref=target,
            send_sem=self.send_sems.at[number],
            recv_sem=self.recv_sems.at[number],
            device_id=device,
            device_id_type=MESH,
        )
        self.copies.append(made)
        return made

    def drain(self):
        for made in self.copies:
            made.wait_send()


def block_rows(first, second, one, two, half):
    block = first.at(one) * first.stride + second.at(two) * second.stride
    start = block * 32 + (0 if half is None else 16 * half)
    size = 32 if half is None else 16
    return pl.ds(pl.multiple_of(start, size), size)


def gather_events(links, buffer, columns, first, second):
    def message(ring, step, one, two, half=None):
        part = buffer.at[block_rows(first, second, one, two, half), columns]
        return links.copy(part, part, ring.to(step))

    ahead, back = message(first, 1, 0, 0), message(first, -1, 0, 0)
    ahead_far, back_far = message(first, 1, -1, 0, 0), message(first, -1, 1, 0, 1)
    near, far = {}, {}
    for one in (0, -1, 1, 2):
        near[one] = message(second, 1, one, 0), message(second, -1, one, 0)
        far[one] = message(second, 1, one, -1, 0), message(second, -1, one, 1, 1)

    def begin():
        for made in (ahead, back) + near[0]:
            made.start()

    def from_behind():
        ahead.wait_recv()
        for made in (ahead_far,) + near[-1]:
            made.start()

    def from_ahead():
        back.wait_recv()
        for made in (back_far,) + near[1]:
            made.start()

    def from_across():
        ahead_far.wait_recv()
        back_far.wait_recv()
        for made in near[2]:
            made.start()

    def onward(one):
        def event():
            for arrived, following in zip(near[one], far[one]):
                arrived.wait_recv()
                following.start()

        return event

    def end():
        for pair in far.values():
            for made in pair:
                made.wait_recv()

    return [begin, from_behind, from_ahead, onward(0), from_across, onward(-1), onward(1), onward(2), end]


def add_to(target, *others):
    total = target[...].astype(F32)
    for other in others:
        total = total + other[...].astype(F32)
    target[...] = total.astype(target.dtype)


class RingSum:
    def __init__(self, links, ring, piece, first, second):
        self.piece, self.first, self.second = piece, first, second
        ahead, back = ring.to(1), ring.to(-1)
        self.far = (
            links.copy(piece(2, 0), first(0), ahead),
            links.copy(piece(2, 1), first(1), back),
        )
        self.own = (
            links.copy(piece(1, 1), second(0, 1), ahead),
            links.copy(piece(-1, 0), second(1, 0), back),
        )
        self.summed = (
            links.copy(piece(1, 0), second(0, 0), ahead),
            links.copy(piece(-1, 1), second(1, 1), back),
        )

    def begin_far(self):
        for made in self.far:
            made.start()

    def begin_own(self):
        for made in self.own:
            made.start()

    def begin(self):
        self.begin_far()
        self.begin_own()

    def onward(self):
        for side, target in enumerate((self.piece(1, 0), self.piece(-1, 1))):
            self.far[side].wait_recv()
            add_to(target, self.first(side))
            self.summed[side].start()

    def end(self):
        for made in self.own + self.summed:
            made.wait_recv()
        for half in range(2):
            add_to(self.piece(0, half), self.second(0, half), self.second(1, half))


def scatter_events(links, buffer, columns, first, second, land1, land2):
    def over_first(slot, two):
        return RingSum(
            links,
            first,
            lambda one, half: buffer.at[block_rows(first, second, one, two, half), columns],
            lambda side: land1.at[slot, side, :, columns],
            lambda side, half: land2.at[slot, side, 16 * half : 16 * half + 16, columns],
        )

    rows = [over_first(slot, two) for slot, two in enumerate((2, -1, 1, 0))]
    column = RingSum(
        links,
        second,
        lambda two, half: buffer.at[block_rows(first, second, 0, two, half), columns],
        lambda side: land1.at[4, side, :, columns],
        lambda side, half: land2.at[4, side, 16 * half : 16 * half + 16, columns],
    )

    def begin():
        for row in rows:
            row.begin()

    def end_far():
        rows[0].end()
        column.begin_far()

    def end_near():
        rows[1].end()
        rows[2].end()
        column.begin_own()

    return [begin] + [row.onward for row in rows] + [end_far, end_near, rows[3].end, column.onward, column.end]


def side_by_side(*lists):
    def together(events):
        def event():
            for each in events:
                each()

        return event

    return [together(events) for events in zip(*lists)]


def softmax_rows(scores):
    shifted = jnp.exp(scores - jnp.max(scores, axis=-1, keepdims=True))
    return shifted / jnp.sum(shifted, axis=-1, keepdims=True)


def same_block():
    rows = lax.broadcasted_iota(jnp.int32, (HD, HD), 0)
    columns = lax.broadcasted_iota(jnp.int32, (HD, HD), 1)
    return (rows >> 5) == (columns >> 5)


def kernel(
    tokens_hbm, cotangent_hbm, shift_hbm, scale_hbm, gate_hbm, w_hbm, mixed, grad_tokens, dw,
    tokens, cotangent, shift, scale, gate, normed_in, scaled_in, branch_in, grad_in,
    land_normed, land_scaled, stage, parted, raw, stage_w,
    xall, w, qkv, grad_att, dall, turned, probs, branch, grad, dpart,
    land1b, land2b, land1g, land2g, land_core, land1y, land2y, land_z, flipped, core_out, core_in,
    send_sems, recv_sems, local_sems, out_sems, in_sems,
):
    f, m = lax.axis_index("frame"), lax.axis_index("mp")
    x, z = lax.rem(m, 4), lax.div(m, 4)
    core, y, zl = lax.rem(f, 2), lax.rem(lax.div(f, 2), 4), lax.div(f, 8)
    other = 1 - core
    ring_x = Ring(x, lambda to: (f, z * 4 + to), 1)
    ring_z = Ring(z, lambda to: (f, to * 4 + x), 4)
    ring_y = Ring(y, lambda to: (zl * 8 + to * 2 + core, m), 0)
    z_partner = ((1 - zl) * 8 + y * 2 + core, m)
    core_partner = (zl * 8 + y * 2 + other, m)
    links = Links(send_sems, recv_sems)

    own_rows = pl.ds(pl.multiple_of(m * 32, 32), 32)
    inputs = [
        pltpu.make_async_copy(source, target, local_sems.at[5 + number])
        for number, (source, target) in enumerate(
            (
                (tokens_hbm, tokens),
                (cotangent_hbm, cotangent),
                (shift_hbm, shift),
                (scale_hbm, scale),
                (gate_hbm, gate),
            )
        )
    ]
    for made in inputs:
        made.start()
    barrier = pltpu.get_barrier_semaphore()
    for ring in (ring_x, ring_z):
        for step in (1, -1):
            pl.semaphore_signal(barrier, inc=1, device_id=ring.to(step), device_id_type=MESH)

    @pl.loop(1, 16)
    def _(step):
        pl.semaphore_signal(
            barrier, inc=1, device_id=(lax.rem(f + step, 16), m), device_id_type=MESH
        )

    weigh = pltpu.make_async_copy(w_hbm, raw, local_sems.at[4])
    weigh.start()
    for made in inputs:
        made.wait()

    def unit_rows(part):
        values = tokens[part].astype(F32)
        inverse_rms = lax.rsqrt(jnp.mean(values * values, axis=-1, keepdims=True) + EPSILON)
        return values * inverse_rms, inverse_rms

    @pl.loop(0, 8)
    def _(patch):
        for clip in range(2):
            part = 2 * patch + clip
            unit, _ = unit_rows(part)
            normed_in[part] = (unit * (1.0 + scale[clip]) + shift[clip]).astype(BF16)
            scaled_in[part] = (cotangent[part].astype(F32) * gate[clip]).astype(BF16)

    def mix():
        @pl.loop(0, 8)
        def _(patch):
            for clip in range(2):
                part = 2 * patch + clip
                mixed[part] = (
                    tokens[part].astype(F32) + gate[clip] * branch_in[part].astype(F32)
                ).astype(BF16)

    def grad_back():
        @pl.loop(0, 8)
        def _(patch):
            for clip in range(2):
                part = 2 * patch + clip
                unit, inverse_rms = unit_rows(part)
                grad_unit = grad_in[part].astype(F32) * (1.0 + scale[clip])
                correction = jnp.mean(grad_unit * unit, axis=-1, keepdims=True)
                grad_tokens[part] = (
                    cotangent[part].astype(F32) + inverse_rms * (grad_unit - unit * correction)
                ).astype(BF16)

    pl.semaphore_wait(barrier, 19)

    def exchange(number, source, target):
        def copy(step):
            to = lax.rem(f + step, 16)
            return pltpu.make_async_remote_copy(
                src_ref=source.at[to],
                dst_ref=target.at[f],
                send_sem=out_sems.at[number, step - 1],
                recv_sem=in_sems.at[number, step - 1],
                device_id=(to, m),
                device_id_type=MESH,
            )

        def here():
            return pltpu.make_async_copy(source.at[f], target.at[f], local_sems.at[number])

        def begin():
            @pl.loop(1, 16)
            def _(step):
                copy(step).start()

            here().start()

        def end():
            @pl.loop(1, 16)
            def _(step):
                copy(step).wait()

            here().wait()

        return begin, end

    def assemble(landed, base):
        for part in range(16):
            stage[2 * part : 2 * part + 2, :] = landed[part].astype(F32)
        xall[own_rows, base : base + D] = stage[...].astype(BF16)

    def part_rows(buffer, number):
        stage[...] = buffer[own_rows, :].astype(F32)
        for part in range(16):
            parted[number, part] = stage[2 * part : 2 * part + 2, :].astype(BF16)

    normed_begin, normed_end = exchange(0, normed_in, land_normed)
    scaled_begin, scaled_end = exchange(1, scaled_in, land_scaled)
    branch_begin, branch_end = exchange(2, parted.at[0], branch_in)
    grad_begin, grad_end = exchange(3, parted.at[1], grad_in)

    def arrange(first, last):
        def event():
            @pl.loop(first, last)
            def _(part):
                stage_w[...] = raw[pl.ds(pl.multiple_of(part * 512, 512), 512), :].astype(F32)
                rows = pl.ds(pl.multiple_of(part * 64, 64), 64)
                for half in range(2):
                    for slot in range(4):
                        place = slot * 256 + half * HD
                        w[rows, place : place + HD] = stage_w[
                            pl.ds(4 * half + slot, 64, stride=8), :
                        ].astype(BF16)

        return event

    def gather(base):
        return side_by_side(
            gather_events(links, xall, slice(base, base + SPLIT), ring_z, ring_x),
            gather_events(links, xall, slice(base + SPLIT, base + D), ring_x, ring_z),
        )

    def scatter(buffer, land1, land2):
        return side_by_side(
            scatter_events(links, buffer, slice(0, SPLIT), ring_x, ring_z, land1, land2),
            scatter_events(links, buffer, slice(SPLIT, D), ring_z, ring_x, land1, land2),
        )

    normed, scaled = gather(0), gather(D)
    sum_branch, sum_grad = scatter(branch, land1b, land2b), scatter(grad, land1g, land2g)

    def chip_columns(y_to, zl_to):
        return pl.ds(pl.multiple_of(zl_to * 1536 + y_to * 384, 128), 384)

    mine = pl.multiple_of(core * 512, 512)
    theirs = pl.multiple_of(other * 512, 512)
    chunks = [(step, side) for side in (1, 0) for step in (2, 1, -1, 0)]
    core_copies = {}
    for step, side in chunks:
        columns = chip_columns(ring_y.at(step), lax.rem(zl + side, 2))
        core_copies[step, side] = links.copy(
            dpart.at[pl.ds(theirs, 512), columns], land_core.at[:, columns], core_partner
        )

    def over_y(side):
        zl_to = lax.rem(zl + side, 2)
        return RingSum(
            links,
            ring_y,
            lambda step, half: dpart.at[
                pl.ds(pl.multiple_of(mine + 256 * half, 256), 256), chip_columns(ring_y.at(step), zl_to)
            ],
            lambda go: land1y.at[side, go],
            lambda go, half: land2y.at[side, go, 256 * half : 256 * half + 256],
        )

    y_sums = [over_y(0), over_y(1)]
    z_copy = links.copy(
        dpart.at[pl.ds(mine, 512), chip_columns(y, 1 - zl)], land_z, z_partner
    )
    core_copy = links.copy(core_out, core_in, core_partner)

    def project(slot):
        qkv[:, 256 * slot : 256 * slot + 256] = dot(
            xall[:, :D], w[:, 256 * slot : 256 * slot + 256]
        ).astype(BF16)

    def attend():
        mask = same_block()

        @pl.loop(0, 4)
        def _(group):
            rows = pl.ds(pl.multiple_of(group * HD, HD), HD)
            for head in range(2):
                query = qkv[rows, head * HD : head * HD + HD]
                key = qkv[rows, 256 + head * HD : 256 + head * HD + HD]
                value = qkv[rows, 512 + head * HD : 512 + head * HD + HD]
                scores = dot(query, key, NT) * (HD ** -0.5)
                attention = softmax_rows(jnp.where(mask, scores, -1e30))
                probs[group * 2 + head] = attention
                dall[rows, 768 + head * HD : 768 + head * HD + HD] = dot(
                    attention.astype(BF16), value
                ).astype(BF16)

    def branch_part(step):
        rows = pl.ds(pl.multiple_of(step * 512, 512), 512)
        branch[:, rows] = dot(dall[:, 768:], w[rows, 768:], NT).astype(BF16)

    def all_branch():
        pl.loop(0, 6)(branch_part)

    def back_project():
        grad_att[...] = dot(xall[:, D:], w[:, 768:]).astype(BF16)

    def attend_back():
        @pl.loop(0, 4)
        def _(group):
            rows = pl.ds(pl.multiple_of(group * HD, HD), HD)
            for head in range(2):
                low = slice(head * HD, head * HD + HD)
                query = qkv[rows, head * HD : head * HD + HD]
                key = qkv[rows, 256 + head * HD : 256 + head * HD + HD]
                value = qkv[rows, 512 + head * HD : 512 + head * HD + HD]
                incoming = grad_att[rows, low]
                attention = probs[group * 2 + head]
                grad_probs = dot(incoming, value, NT)
                inner = jnp.sum(grad_probs * attention, axis=-1, keepdims=True)
                grad_scores = (attention * (grad_probs - inner) * (HD ** -0.5)).astype(BF16)
                dall[rows, head * HD : head * HD + HD] = dot(grad_scores, key).astype(BF16)
                dall[rows, 256 + head * HD : 256 + head * HD + HD] = dot(
                    grad_scores, query, TN
                ).astype(BF16)
                dall[rows, 512 + head * HD : 512 + head * HD + HD] = dot(
                    attention.astype(BF16), incoming, TN
                ).astype(BF16)

    def grad_part(step):
        rows = pl.ds(pl.multiple_of(step * 512, 512), 512)
        grad[:, rows] = dot(dall[:, :768], w[rows, :768], NT).astype(BF16)

    def all_grad():
        pl.loop(0, 6)(grad_part)

    def turn():
        for part in range(8):
            turned[part * HD : part * HD + HD, :] = dall[:, part * HD : part * HD + HD].T

    def weight_chunk(step, side):
        def event():
            zl_to = lax.rem(zl + side, 2)
            columns = chip_columns(ring_y.at(step), zl_to)
            gated = pl.ds(pl.multiple_of(D + zl_to * 1536 + ring_y.at(step) * 384, 128), 384)
            dpart[:768, columns] = dot(turned[:768, :], xall[:, columns]).astype(BF16)
            dpart[768:, columns] = dot(turned[768:, :], xall[:, gated]).astype(BF16)
            core_copies[step, side].start()

        return event

    def core_sum(step, side):
        def event():
            columns = chip_columns(ring_y.at(step), lax.rem(zl + side, 2))
            core_copies[step, side].wait_recv()
            add_to(dpart.at[pl.ds(mine, 512), columns], land_core.at[:, columns])

        return event

    def z_end():
        z_copy.wait_recv()
        columns = chip_columns(y, zl)
        total = dpart[pl.ds(mine, 512), columns].astype(F32) + land_z[...].astype(F32)
        flipped[...] = total.T
        core_out[...] = flipped[pl.ds(pl.multiple_of(other * 192, 192), 192), :].astype(BF16)
        core_copy.start()
        give(2 * core, flipped[pl.ds(pl.multiple_of(core * 192, 192), 192), :])

    def give(slot, values):
        for number in range(4):
            place = pl.ds(4 * (number % 2) + slot + number // 2, 192, stride=8)
            dw[place, :] = values[:, number * HD : number * HD + HD]

    def core_end():
        core_copy.wait_recv()
        give(2 * other, core_in[...].astype(F32))

    n, s, b, g = normed, scaled, sum_branch, sum_grad
    plan = [
        normed_begin, scaled_begin, normed_end, lambda: assemble(land_normed, 0),
        n[0],
        scaled_end, lambda: assemble(land_scaled, D),
        weigh.wait, n[1], n[2], arrange(0, 8), n[3], n[4], arrange(8, 16), s[0], n[5], arrange(16, 24), n[6],
        arrange(24, 32), n[7], arrange(32, 40), s[1], s[2], arrange(40, 48), n[8],
        lambda: project(0), s[3], lambda: project(1), s[4], lambda: project(2), s[5],
        attend, s[6], all_branch, s[7], b[0],
        s[8],
        back_project, b[1], attend_back, b[2], turn,
        *[weight_chunk(*chunk) for chunk in chunks[:4]], b[3],
        *[weight_chunk(*chunk) for chunk in chunks[4:]], b[4],
        all_grad, g[0], b[5], b[6],
        *[core_sum(*chunk) for chunk in chunks[:4]], y_sums[1].begin,
        b[7],
        *[core_sum(*chunk) for chunk in chunks[4:]], y_sums[0].begin,
        b[8], g[1], g[2],
        y_sums[1].onward,
        b[9], lambda: part_rows(branch, 0), branch_begin,
        g[3], g[4], y_sums[0].onward,
        g[5], g[6], g[7],
        y_sums[1].end, z_copy.start,
        g[8],
        y_sums[0].end, z_end,
        g[9], lambda: part_rows(grad, 1), grad_begin,
        core_end,
        branch_end, mix, grad_end, grad_back,
    ]
    for event in plan:
        event()
    links.drain()


def attention_block(tokens, cotangent, shift, scale, gate, weights):
    copies = 224
    return pl.pallas_call(
        kernel,
        out_shape=(
            jax.ShapeDtypeStruct((16, 2, D), BF16),
            jax.ShapeDtypeStruct((16, 2, D), BF16),
            jax.ShapeDtypeStruct((1536, HD), F32),
        ),
        in_specs=[pl.BlockSpec(memory_space=pl.ANY)] * 6,
        out_specs=[pl.BlockSpec(memory_space=pltpu.VMEM)] * 3,
        scratch_shapes=[
            pltpu.VMEM((16, 2, D), BF16),
            pltpu.VMEM((16, 2, D), BF16),
            pltpu.VMEM((2, 2, D), F32),
            pltpu.VMEM((2, 2, D), F32),
            pltpu.VMEM((2, 2, D), F32),
            pltpu.VMEM((16, 2, D), BF16),
            pltpu.VMEM((16, 2, D), BF16),
            pltpu.VMEM((16, 2, D), BF16),
            pltpu.VMEM((16, 2, D), BF16),
            pltpu.VMEM((16, 2, D), BF16),
            pltpu.VMEM((16, 2, D), BF16),
            pltpu.VMEM((32, D), F32),
            pltpu.VMEM((2, 16, 2, D), BF16),
            pltpu.VMEM((24576, HD), BF16),
            pltpu.VMEM((512, HD), F32),
            pltpu.VMEM((512, 2 * D), BF16),
            pltpu.VMEM((D, 1024), BF16),
            pltpu.VMEM((512, 768), BF16),
            pltpu.VMEM((512, 256), BF16),
            pltpu.VMEM((512, 1024), BF16),
            pltpu.VMEM((1024, 512), BF16),
            pltpu.VMEM((8, HD, HD), F32),
            pltpu.VMEM((512, D), BF16),
            pltpu.VMEM((512, D), BF16),
            pltpu.VMEM((1024, D), BF16),
            pltpu.VMEM((5, 2, 16, D), BF16),
            pltpu.VMEM((5, 2, 32, D), BF16),
            pltpu.VMEM((5, 2, 16, D), BF16),
            pltpu.VMEM((5, 2, 32, D), BF16),
            pltpu.VMEM((512, D), BF16),
            pltpu.VMEM((2, 2, 256, 384), BF16),
            pltpu.VMEM((2, 2, 512, 384), BF16),
            pltpu.VMEM((512, 384), BF16),
            pltpu.VMEM((384, 512), F32),
            pltpu.VMEM((192, 512), BF16),
            pltpu.VMEM((192, 512), BF16),
            pltpu.SemaphoreType.DMA((copies,)),
            pltpu.SemaphoreType.DMA((copies,)),
            pltpu.SemaphoreType.DMA((10,)),
            pltpu.SemaphoreType.DMA((4, 15)),
            pltpu.SemaphoreType.DMA((4, 15)),
        ],
        compiler_params=pltpu.CompilerParams(
            collective_id=0, has_side_effects=True, vmem_limit_bytes=60 * MIB
        ),
    )(tokens, cotangent, shift, scale, gate, weights)


def on_device(tokens, cotangent, mod_shift, mod_scale, mod_gate, attn_weights):
    weights = attn_weights.reshape(D, 4, 2, HD).transpose(0, 2, 1, 3).reshape(8 * D, HD)
    mixed, grad_tokens, weight_grads = attention_block(
        tokens.reshape(16, 2, D), cotangent.reshape(16, 2, D), mod_shift, mod_scale, mod_gate, weights
    )
    weight_grads = weight_grads.reshape(192, 2, 4, HD).transpose(0, 2, 1, 3).reshape(192, 4, 256)
    return mixed.reshape(tokens.shape), grad_tokens.reshape(tokens.shape), weight_grads


def solution(mesh):
    placed = (
        P("mp", None, "frame", None),
        P("mp", None, "frame", None),
        P(None, "frame", None),
        P(None, "frame", None),
        P(None, "frame", None),
        P(None, None, "mp"),
    )
    return jax.shard_map(
        on_device,
        mesh=mesh,
        in_specs=placed,
        out_specs=(
            P("mp", None, "frame", None),
            P("mp", None, "frame", None),
            P("frame", None, "mp"),
        ),
        check_vma=False,
    )
```

```python
from types import SimpleNamespace

import jax
import jax.numpy as jnp
from jax import lax
from jax.experimental import pallas as pl
from jax.experimental.pallas import tpu as pltpu
from jax.sharding import PartitionSpec as P

HD = 128
D = 3072
EPSILON = 1e-06
MESH = pl.DeviceIdType.MESH
BF16 = jnp.bfloat16
F32 = jnp.float32
MIB = 1024 * 1024
SPLIT = 2432


def dot(a, b, dims=((1,), (0,))):
    return lax.dot_general(a, b, (dims, ((), ())), preferred_element_type=F32)


NT = ((1,), (1,))
TN = ((0,), (0,))


class Ring:
    def __init__(self, index, device, stride):
        self.index, self.device, self.stride = index, device, stride

    def at(self, step):
        return lax.rem(self.index + (step + 4), 4)

    def to(self, step):
        return self.device(self.at(step))


class Links:
    def __init__(self, send_sems, recv_sems):
        self.send_sems, self.recv_sems = send_sems, recv_sems
        self.groups, self.sends = 0, []

    def send_group(self, whole):
        self.sends.append(whole)
        return len(self.sends) - 1

    def recv_group(self):
        self.groups += 1
        return self.groups - 1

    def copy(self, source, target, device, send, recv):
        return pltpu.make_async_remote_copy(
            src_ref=source,
            dst_ref=target,
            send_sem=self.send_sems.at[send],
            recv_sem=self.recv_sems.at[recv],
            device_id=device,
            device_id_type=MESH,
        )

    def wait(self, recv, whole):
        pltpu.make_async_copy(whole, whole, self.recv_sems.at[recv]).wait()

    def drain(self):
        for send, whole in enumerate(self.sends):
            pltpu.make_async_copy(whole, whole, self.send_sems.at[send]).wait()


def block_rows(first, second, one, two, half):
    block = first.at(one) * first.stride + second.at(two) * second.stride
    start = block * 32 + (0 if half is None else 16 * half)
    size = 32 if half is None else 16
    return pl.ds(pl.multiple_of(start, size), size)


def gather_steps(links, send, buffer, columns, first, second):
    class Group:
        def __init__(self, rows, *moves):
            self.whole, self.recv = buffer.at[0:rows, columns], links.recv_group()
            self.copies = []
            for ring, step, one, two, half in moves:
                part = buffer.at[block_rows(first, second, one, two, half), columns]
                self.copies.append(links.copy(part, part, ring.to(step), send, self.recv))

        def start(self):
            for made in self.copies:
                made.start()

        def wait(self):
            links.wait(self.recv, self.whole)

    places = (0, -1, 1, 2)
    ahead = Group(32, (first, 1, 0, 0, None))
    back = Group(32, (first, -1, 0, 0, None))
    across = Group(32, (first, 1, -1, 0, 0), (first, -1, 1, 0, 1))
    near = {one: Group(64, (second, 1, one, 0, None), (second, -1, one, 0, None)) for one in places}
    far = Group(
        128, *[move for one in places for move in ((second, 1, one, -1, 0), (second, -1, one, 1, 1))]
    )

    def begin():
        for group in (ahead, back, near[0]):
            group.start()

    def from_behind():
        ahead.wait()
        across.copies[0].start()
        near[-1].start()

    def from_ahead():
        back.wait()
        across.copies[1].start()
        near[1].start()

    def from_across():
        across.wait()
        near[2].start()

    def onward(place):
        def event():
            near[places[place]].wait()
            far.copies[2 * place].start()
            far.copies[2 * place + 1].start()

        return event

    return SimpleNamespace(
        begin=begin,
        behind=from_behind,
        ahead=from_ahead,
        across=from_across,
        on_own=onward(0),
        on_behind=onward(1),
        on_ahead=onward(2),
        on_across=onward(3),
        end=far.wait,
    )


def add_to(target, *others):
    total = target[...].astype(F32)
    for other in others:
        total = total + other[...].astype(F32)
    target[...] = total.astype(target.dtype)


class RingSum:
    def __init__(self, links, send, ring, piece, first, second):
        self.links, self.piece, self.first, self.second = links, piece, first, second
        ahead, back = ring.to(1), ring.to(-1)
        self.early, self.late = links.recv_group(), links.recv_group()

        def copy(source, target, device, recv):
            return links.copy(source, target, device, send, recv)

        self.far = (
            copy(piece(2, 0), first(0), ahead, self.early),
            copy(piece(2, 1), first(1), back, self.early),
        )
        self.own = (
            copy(piece(1, 1), second(0, 1), ahead, self.late),
            copy(piece(-1, 0), second(1, 0), back, self.late),
        )
        self.summed = (
            copy(piece(1, 0), second(0, 0), ahead, self.late),
            copy(piece(-1, 1), second(1, 1), back, self.late),
        )

    def begin_far(self):
        for made in self.far:
            made.start()

    def begin_own(self):
        for made in self.own:
            made.start()

    def onward(self):
        self.links.wait(self.early, self.first(None))
        for side, target in enumerate((self.piece(1, 0), self.piece(-1, 1))):
            add_to(target, self.first(side))
            self.summed[side].start()

    def end(self):
        self.links.wait(self.late, self.second(None, None))
        for half in range(2):
            add_to(self.piece(0, half), self.second(0, half), self.second(1, half))


def sides(land, *rest):
    def view(side, half=None):
        if side is None:
            return land.at[(slice(None), slice(None), *rest)]
        if half is None:
            return land.at[(side, slice(None), *rest)]
        size = land.shape[1] // 2
        return land.at[(side, slice(size * half, size * half + size), *rest)]

    return view


def scatter_steps(links, send, buffer, columns, first, second, land1, land2):
    def over_first(slot, two):
        return RingSum(
            links,
            send,
            first,
            lambda one, half: buffer.at[block_rows(first, second, one, two, half), columns],
            sides(land1.at[slot], columns),
            sides(land2.at[slot], columns),
        )

    rows = [over_first(slot, two) for slot, two in enumerate((2, -1, 1, 0))]
    column = RingSum(
        links,
        send,
        second,
        lambda two, half: buffer.at[block_rows(first, second, 0, two, half), columns],
        sides(land1.at[4], columns),
        sides(land2.at[4], columns),
    )

    return [*rows, column]


def softmax_rows(scores):
    shifted = jnp.exp(scores - jnp.max(scores, axis=-1, keepdims=True))
    return shifted / jnp.sum(shifted, axis=-1, keepdims=True)


def same_block():
    rows = lax.broadcasted_iota(jnp.int32, (HD, HD), 0)
    columns = lax.broadcasted_iota(jnp.int32, (HD, HD), 1)
    return (rows >> 5) == (columns >> 5)


def kernel(
    tokens_hbm, cotangent_hbm, shift_hbm, scale_hbm, gate_hbm, w_hbm, mixed, grad_tokens, dw,
    tokens, cotangent, shift, scale, gate, normed_in, scaled_in, branch_in, grad_in,
    land_normed, land_scaled, stage, parted, raw, stage_w,
    xall, w, qkv, grad_att, dall, turned, probs, branch, grad, dpart,
    land1b, land2b, land1g, land2g, land_core, land1y, land2y, land_z, flipped, core_out, core_in,
    send_sems, recv_sems, local_sems, out_sems, in_sems,
):
    f, m = lax.axis_index("frame"), lax.axis_index("mp")
    x, z = lax.rem(m, 4), lax.div(m, 4)
    core, y, zl = lax.rem(f, 2), lax.rem(lax.div(f, 2), 4), lax.div(f, 8)
    other = 1 - core
    ring_x = Ring(x, lambda to: (f, z * 4 + to), 1)
    ring_z = Ring(z, lambda to: (f, to * 4 + x), 4)
    ring_y = Ring(y, lambda to: (zl * 8 + to * 2 + core, m), 0)
    z_partner = ((1 - zl) * 8 + y * 2 + core, m)
    core_partner = (zl * 8 + y * 2 + other, m)
    links = Links(send_sems, recv_sems)

    own_rows = pl.ds(pl.multiple_of(m * 32, 32), 32)
    inputs = [
        pltpu.make_async_copy(source, target, local_sems.at[5 + number])
        for number, (source, target) in enumerate(
            (
                (tokens_hbm, tokens),
                (cotangent_hbm, cotangent),
                (shift_hbm, shift),
                (scale_hbm, scale),
                (gate_hbm, gate),
            )
        )
    ]
    for made in inputs:
        made.start()
    barrier = pltpu.get_barrier_semaphore()
    for ring in (ring_x, ring_z):
        for step in (1, -1):
            pl.semaphore_signal(barrier, inc=1, device_id=ring.to(step), device_id_type=MESH)

    @pl.loop(1, 16)
    def _(step):
        pl.semaphore_signal(
            barrier, inc=1, device_id=(lax.rem(f + step, 16), m), device_id_type=MESH
        )

    weigh = pltpu.make_async_copy(w_hbm, raw, local_sems.at[4])
    weigh.start()
    for made in inputs:
        made.wait()

    def total(values):
        eight = values[0:8]
        for tile in range(1, 6):
            eight = eight + values[8 * tile : 8 * tile + 8]
        eight = eight + pltpu.roll(eight, 2, 0)
        eight = eight + pltpu.roll(eight, 4, 0)
        eight = jnp.sum(eight, axis=-1, keepdims=True)
        return jnp.concatenate([eight] * 6, axis=0)

    def part_of(patch, clip):
        return pl.ds(pl.multiple_of((2 * patch + clip) * 48, 48), 48)

    def of_clip(clip):
        return slice(48 * clip, 48 * clip + 48)

    def unit_rows(rows):
        values = tokens[rows, :].astype(F32)
        inverse_rms = lax.rsqrt(total(values * values) * (1.0 / D) + EPSILON)
        return values * inverse_rms, inverse_rms

    @pl.loop(0, 8)
    def _(patch):
        for clip in range(2):
            rows, own = part_of(patch, clip), of_clip(clip)
            unit, _ = unit_rows(rows)
            normed_in[rows, :] = (unit * (1.0 + scale[own, :]) + shift[own, :]).astype(BF16)
            scaled_in[rows, :] = (cotangent[rows, :].astype(F32) * gate[own, :]).astype(BF16)

    def mix():
        @pl.loop(0, 8)
        def _(patch):
            for clip in range(2):
                rows, own = part_of(patch, clip), of_clip(clip)
                mixed[rows, :] = (
                    tokens[rows, :].astype(F32) + gate[own, :] * branch_in[rows, :].astype(F32)
                ).astype(mixed.dtype)

    def grad_back():
        @pl.loop(0, 8)
        def _(patch):
            for clip in range(2):
                rows, own = part_of(patch, clip), of_clip(clip)
                unit, inverse_rms = unit_rows(rows)
                grad_unit = grad_in[rows, :].astype(F32) * (1.0 + scale[own, :])
                correction = total(grad_unit * unit) * (1.0 / D)
                grad_tokens[rows, :] = (
                    cotangent[rows, :].astype(F32) + inverse_rms * (grad_unit - unit * correction)
                ).astype(grad_tokens.dtype)

    pl.semaphore_wait(barrier, 19)

    def exchange(number, source, target):
        def part(index):
            return pl.ds(pl.multiple_of(index * 48, 48), 48)

        def copy(step):
            to = lax.rem(f + step, 16)
            return pltpu.make_async_remote_copy(
                src_ref=source.at[part(to)],
                dst_ref=target.at[part(f)],
                send_sem=out_sems.at[number],
                recv_sem=in_sems.at[number],
                device_id=(to, m),
                device_id_type=MESH,
            )

        def here():
            return pltpu.make_async_copy(source.at[part(f)], target.at[part(f)], local_sems.at[number])

        def begin():
            @pl.loop(1, 16)
            def _(step):
                copy(step).start()

            here().start()

        def end():
            pltpu.make_async_copy(target.at[0:720], target.at[0:720], in_sems.at[number]).wait()
            here().wait()

        def sent():
            pltpu.make_async_copy(source.at[0:720], source.at[0:720], out_sems.at[number]).wait()

        sent_all.append(sent)
        return begin, end

    def assemble(landed, base):
        stage[...] = landed[...].astype(F32)
        for tile in range(24):
            for frame in range(2):
                xall[
                    pl.ds(pl.multiple_of(m * 32 + 16 * frame, 16), 16),
                    base + HD * tile : base + HD * tile + HD,
                ] = stage[pl.ds(2 * tile + frame, 16, stride=48), :].astype(BF16)

    def part_rows(buffer, number):
        for tile in range(24):
            for frame in range(2):
                stage[pl.ds(2 * tile + frame, 16, stride=48), :] = buffer[
                    pl.ds(pl.multiple_of(m * 32 + 16 * frame, 16), 16), HD * tile : HD * tile + HD
                ].astype(F32)
        parted[number] = stage[...].astype(BF16)

    sent_all = []
    normed_begin, normed_end = exchange(0, normed_in, land_normed)
    scaled_begin, scaled_end = exchange(1, scaled_in, land_scaled)
    branch_begin, branch_end = exchange(2, parted.at[0], branch_in)
    grad_begin, grad_end = exchange(3, parted.at[1], grad_in)

    def arrange(first, last):
        def event():
            @pl.loop(first, last)
            def _(part):
                stage_w[...] = raw[pl.ds(pl.multiple_of(part * 512, 512), 512), :].astype(F32)
                rows = pl.ds(pl.multiple_of(part * 64, 64), 64)
                for half in range(2):
                    for slot in range(4):
                        place = slot * 256 + half * HD
                        w[rows, place : place + HD] = stage_w[
                            pl.ds(4 * half + slot, 64, stride=8), :
                        ].astype(BF16)

        return event

    early, late = slice(0, SPLIT), slice(SPLIT, D)

    def gather(base):
        send = links.send_group(xall.at[0:480, base : base + D])
        return (
            gather_steps(links, send, xall, slice(base, base + SPLIT), ring_z, ring_x),
            gather_steps(links, send, xall, slice(base + SPLIT, base + D), ring_x, ring_z),
        )

    def scatter(buffer, *lands):
        send = links.send_group(buffer.at[0:480, :])
        return (
            scatter_steps(links, send, buffer, early, ring_x, ring_z, *lands),
            scatter_steps(links, send, buffer, late, ring_z, ring_x, *lands),
        )

    (na, nb), (sa, sb) = gather(0), gather(D)
    ba, bb = scatter(branch, land1b, land2b)
    ga, gb = scatter(grad, land1g, land2g)

    def chip_columns(y_to, zl_to):
        return pl.ds(pl.multiple_of(zl_to * 1536 + y_to * 384, 128), 384)

    mine = pl.multiple_of(core * 512, 512)
    theirs = pl.multiple_of(other * 512, 512)
    chunks = [(step, side) for side in (1, 0) for step in (2, 1, -1, 0)]
    core_copies, core_sends, first_core = {}, links.send_group(land_core), links.groups
    for step, side in chunks:
        columns = chip_columns(ring_y.at(step), lax.rem(zl + side, 2))
        core_copies[step, side] = links.copy(
            dpart.at[pl.ds(theirs, 512), columns], land_core.at[:, columns], core_partner,
            core_sends, links.recv_group(),
        )

    def over_y(side):
        zl_to = lax.rem(zl + side, 2)
        return RingSum(
            links,
            links.send_group(dpart.at[0:768, 0:768]),
            ring_y,
            lambda step, half: dpart.at[
                pl.ds(pl.multiple_of(mine + 256 * half, 256), 256), chip_columns(ring_y.at(step), zl_to)
            ],
            sides(land1y.at[side]),
            sides(land2y.at[side]),
        )

    y_sums = [over_y(0), over_y(1)]
    z_recv, core_recv = links.recv_group(), links.recv_group()
    z_copy = links.copy(
        dpart.at[pl.ds(mine, 512), chip_columns(y, 1 - zl)], land_z, z_partner,
        links.send_group(land_z), z_recv,
    )
    core_copy = links.copy(
        core_out, core_in, core_partner, links.send_group(core_in), core_recv
    )

    def project(slot):
        qkv[:, 256 * slot : 256 * slot + 256] = dot(
            xall[:, :D], w[:, 256 * slot : 256 * slot + 256]
        ).astype(BF16)

    def attend(group):
        def event():
            mask = same_block()
            rows = slice(group * HD, group * HD + HD)
            for head in range(2):
                query = qkv[rows, head * HD : head * HD + HD]
                key = qkv[rows, 256 + head * HD : 256 + head * HD + HD]
                value = qkv[rows, 512 + head * HD : 512 + head * HD + HD]
                scores = dot(query, key, NT) * (HD ** -0.5)
                attention = softmax_rows(jnp.where(mask, scores, -1e30))
                probs[group * 2 + head] = attention
                dall[rows, 768 + head * HD : 768 + head * HD + HD] = dot(
                    attention.astype(BF16), value
                ).astype(BF16)

        return event

    def branch_part(part):
        def event():
            @pl.loop(2 * part, 2 * part + 2)
            def _(step):
                rows = pl.ds(pl.multiple_of(step * 512, 512), 512)
                branch[:, rows] = dot(dall[:, 768:], w[rows, 768:], NT).astype(BF16)

        return event

    def back_project():
        grad_att[...] = dot(xall[:, D:], w[:, 768:]).astype(BF16)

    def attend_back(group):
        def event():
            rows = slice(group * HD, group * HD + HD)
            for head in range(2):
                low = slice(head * HD, head * HD + HD)
                query = qkv[rows, head * HD : head * HD + HD]
                key = qkv[rows, 256 + head * HD : 256 + head * HD + HD]
                value = qkv[rows, 512 + head * HD : 512 + head * HD + HD]
                incoming = grad_att[rows, low]
                attention = probs[group * 2 + head]
                grad_probs = dot(incoming, value, NT)
                inner = jnp.sum(grad_probs * attention, axis=-1, keepdims=True)
                grad_scores = (attention * (grad_probs - inner) * (HD ** -0.5)).astype(BF16)
                dall[rows, head * HD : head * HD + HD] = dot(grad_scores, key).astype(BF16)
                dall[rows, 256 + head * HD : 256 + head * HD + HD] = dot(
                    grad_scores, query, TN
                ).astype(BF16)
                dall[rows, 512 + head * HD : 512 + head * HD + HD] = dot(
                    attention.astype(BF16), incoming, TN
                ).astype(BF16)

        return event

    def grad_part(part):
        def event():
            @pl.loop(2 * part, 2 * part + 2)
            def _(step):
                rows = pl.ds(pl.multiple_of(step * 512, 512), 512)
                grad[:, rows] = dot(dall[:, :768], w[rows, :768], NT).astype(BF16)

        return event

    def turn():
        for part in range(8):
            turned[part * HD : part * HD + HD, :] = dall[:, part * HD : part * HD + HD].T

    def weight_chunk(step, side):
        def event():
            zl_to = lax.rem(zl + side, 2)
            columns = chip_columns(ring_y.at(step), zl_to)
            gated = pl.ds(pl.multiple_of(D + zl_to * 1536 + ring_y.at(step) * 384, 128), 384)
            dpart[:768, columns] = dot(turned[:768, :], xall[:, columns]).astype(BF16)
            dpart[768:, columns] = dot(turned[768:, :], xall[:, gated]).astype(BF16)
            core_copies[step, side].start()

        return event

    def core_sum(step, side):
        def event():
            columns = chip_columns(ring_y.at(step), lax.rem(zl + side, 2))
            links.wait(first_core + chunks.index((step, side)), land_core.at[:, columns])
            add_to(dpart.at[pl.ds(mine, 512), columns], land_core.at[:, columns])

        return event

    def z_end():
        links.wait(z_recv, land_z)
        columns = chip_columns(y, zl)
        total = dpart[pl.ds(mine, 512), columns].astype(F32) + land_z[...].astype(F32)
        flipped[...] = total.T
        core_out[...] = flipped[pl.ds(pl.multiple_of(other * 192, 192), 192), :].astype(BF16)
        core_copy.start()
        give(2 * core, flipped[pl.ds(pl.multiple_of(core * 192, 192), 192), :])

    def give(slot, values):
        for number in range(4):
            place = pl.ds(4 * (number % 2) + slot + number // 2, 192, stride=8)
            dw[place, :] = values[:, number * HD : number * HD + HD]

    def core_end():
        links.wait(core_recv, core_in)
        give(2 * other, core_in[...].astype(F32))

    def y_begin(side):
        def event():
            y_sums[side].begin_far()
            y_sums[side].begin_own()

        return event

    def in_turn(*steps):
        def event():
            for step in steps:
                step()

        return event

    take_scaled = in_turn(scaled_end, lambda: assemble(land_scaled, D))
    ar = [arrange(8 * part, 8 * part + 8) for part in range(6)]
    ar[0] = in_turn(weigh.wait, ar[0])
    pr = [lambda slot=slot: project(slot) for slot in range(3)]
    br, gr = ([make(part) for part in range(3)] for make in (branch_part, grad_part))
    at, ab = ([make(part) for part in range(4)] for make in (attend, attend_back))
    wc, cs = ([make(*chunk) for chunk in chunks] for make in (weight_chunk, core_sum))
    y_start = [y_begin(side) for side in range(2)]
    y_on = [each.onward for each in y_sums]
    y_end = [y_sums[0].end, in_turn(y_sums[1].end, z_copy.start)]
    give_branch = in_turn(lambda: part_rows(branch, 0), branch_begin)
    give_grad = in_turn(lambda: part_rows(grad, 1), grad_begin)
    take_branch, take_grad = in_turn(branch_end, mix), in_turn(grad_end, grad_back)

    plan = [
        na.begin, nb.begin, ar[0], ar[1], ar[2], ar[3], ar[4], ar[5], take_scaled, sa.begin, na.on_own,
        nb.behind, nb.ahead, sb.begin, na.ahead, na.behind, sa.on_own, nb.on_own, nb.across, sb.behind,
        sb.ahead, na.on_ahead, sa.behind, sa.ahead, nb.on_behind, na.on_behind, nb.on_ahead, sb.across,
        sb.on_own, na.across, sa.on_behind, nb.on_across, sa.on_ahead, sb.on_behind, sb.on_ahead,
        na.on_across, sa.across, sb.on_across, na.end, nb.end, pr[0], pr[1], pr[2], sa.on_across, at[0],
        at[1], at[2], at[3], br[0], br[1], br[2], ba[1].begin_own, bb[3].begin_own, ba[0].begin_far,
        bb[0].begin_far, ba[2].begin_own, bb[2].begin_far, ba[1].begin_far, ba[0].begin_own, bb[1].begin_far,
        bb[3].begin_far, ba[2].begin_far, bb[2].begin_own, bb[1].begin_own, sb.end, bb[0].begin_own, sa.end,
        back_project, ab[0], ab[1], ab[2], ab[3], gr[0], gr[1], gr[2], gb[3].begin_far, gb[2].begin_own,
        gb[1].begin_far, gb[3].begin_own, gb[2].begin_far, ga[0].begin_far, gb[0].begin_far, gb[1].begin_own,
        turn, wc[0], wc[1], wc[2], ba[0].onward, bb[0].onward, bb[3].onward, ga[0].begin_own, wc[3], wc[4],
        wc[5], ba[2].onward, cs[0], gb[0].begin_own, wc[6], wc[7], cs[1], ga[0].onward, cs[2], gb[1].onward,
        cs[3], y_start[1], ga[2].begin_far, gb[2].onward, cs[4], ba[1].onward, bb[2].onward, cs[5],
        gb[3].onward, ga[1].begin_far, cs[6], ba[0].end, ba[4].begin_far, gb[0].onward, cs[7], y_start[0],
        ga[2].begin_own, bb[0].end, ga[1].begin_own, bb[4].begin_far, bb[1].onward, bb[3].end, ba[2].end,
        gb[1].end, ga[0].end, ga[4].begin_far, gb[2].end, gb[4].begin_own, y_on[1], bb[2].end, ga[2].onward,
        gb[3].end, ba[1].end, ba[4].begin_own, ga[1].onward, ba[4].onward, gb[0].end, gb[4].begin_far,
        bb[1].end, bb[4].begin_own, ba[3].begin_own, bb[4].onward, ga[3].begin_far, y_on[0], ga[3].begin_own,
        ga[2].end, ga[1].end, ga[4].onward, ga[4].begin_own, gb[4].onward, ba[3].begin_far, bb[4].end,
        ga[3].onward, y_end[1], gb[4].end, ba[3].onward, y_end[0], ga[3].end, ga[4].end, give_grad,
        ba[3].end, ba[4].end, give_branch, z_end, take_grad, core_end, take_branch,
    ]
    normed_begin()
    scaled_begin()
    normed_end()
    assemble(land_normed, 0)
    for step in plan:
        step()
    links.drain()
    for sent in sent_all:
        sent()


def attention_block(tokens, cotangent, shift, scale, gate, weights):
    return pl.pallas_call(
        kernel,
        out_shape=(
            jax.ShapeDtypeStruct((768, HD), BF16),
            jax.ShapeDtypeStruct((768, HD), BF16),
            jax.ShapeDtypeStruct((1536, HD), F32),
        ),
        in_specs=[pl.BlockSpec(memory_space=pl.ANY)] * 6,
        out_specs=[pl.BlockSpec(memory_space=pltpu.VMEM)] * 3,
        scratch_shapes=[
            pltpu.VMEM((768, HD), BF16),
            pltpu.VMEM((768, HD), BF16),
            pltpu.VMEM((96, HD), F32),
            pltpu.VMEM((96, HD), F32),
            pltpu.VMEM((96, HD), F32),
            pltpu.VMEM((768, HD), BF16),
            pltpu.VMEM((768, HD), BF16),
            pltpu.VMEM((768, HD), BF16),
            pltpu.VMEM((768, HD), BF16),
            pltpu.VMEM((768, HD), BF16),
            pltpu.VMEM((768, HD), BF16),
            pltpu.VMEM((768, HD), F32),
            pltpu.VMEM((2, 768, HD), BF16),
            pltpu.VMEM((24576, HD), BF16),
            pltpu.VMEM((512, HD), F32),
            pltpu.VMEM((512, 2 * D), BF16),
            pltpu.VMEM((D, 1024), BF16),
            pltpu.VMEM((512, 768), BF16),
            pltpu.VMEM((512, 256), BF16),
            pltpu.VMEM((512, 1024), BF16),
            pltpu.VMEM((1024, 512), BF16),
            pltpu.VMEM((8, HD, HD), F32),
            pltpu.VMEM((512, D), BF16),
            pltpu.VMEM((512, D), BF16),
            pltpu.VMEM((1024, D), BF16),
            pltpu.VMEM((5, 2, 16, D), BF16),
            pltpu.VMEM((5, 2, 32, D), BF16),
            pltpu.VMEM((5, 2, 16, D), BF16),
            pltpu.VMEM((5, 2, 32, D), BF16),
            pltpu.VMEM((512, D), BF16),
            pltpu.VMEM((2, 2, 256, 384), BF16),
            pltpu.VMEM((2, 2, 512, 384), BF16),
            pltpu.VMEM((512, 384), BF16),
            pltpu.VMEM((384, 512), F32),
            pltpu.VMEM((192, 512), BF16),
            pltpu.VMEM((192, 512), BF16),
            pltpu.SemaphoreType.DMA((9,)),
            pltpu.SemaphoreType.DMA((86,)),
            pltpu.SemaphoreType.DMA((10,)),
            pltpu.SemaphoreType.DMA((4,)),
            pltpu.SemaphoreType.DMA((4,)),
        ],
        compiler_params=pltpu.CompilerParams(
            collective_id=0, has_side_effects=True, vmem_limit_bytes=60 * MIB
        ),
    )(tokens, cotangent, shift, scale, gate, weights)


def copy_kernel(*refs):
    half = len(refs) // 2
    for source, target in zip(refs[:half], refs[half:]):
        target[...] = source[...]


def copied(*arrays):
    return pl.pallas_call(
        copy_kernel,
        out_shape=[jax.ShapeDtypeStruct(each.shape, each.dtype) for each in arrays],
        in_specs=[pl.BlockSpec(memory_space=pltpu.VMEM)] * len(arrays),
        out_specs=[pl.BlockSpec(memory_space=pltpu.VMEM)] * len(arrays),
    )(*arrays)


def on_device(tokens, cotangent, mod_shift, mod_scale, mod_gate, attn_weights):
    weights = attn_weights.reshape(D, 4, 2, HD).transpose(0, 2, 1, 3).reshape(8 * D, HD)
    def tiles(values):
        lead = values.shape[:-2]
        return jnp.swapaxes(values.reshape(*lead, 2, 24, HD), -2, -3).reshape(-1, HD)

    def untiled(values):
        return jnp.swapaxes(values.reshape(8, 2, 24, 2, HD), -2, -3).reshape(8, 2, 2, D)

    mixed, grad_tokens, weight_grads = attention_block(
        tiles(tokens), tiles(cotangent), tiles(mod_shift), tiles(mod_scale), tiles(mod_gate), weights
    )
    mixed, grad_tokens, weight_grads = copied(mixed, grad_tokens, weight_grads)
    weight_grads = weight_grads.reshape(192, 2, 4, HD).transpose(0, 2, 1, 3).reshape(192, 4, 256)
    return untiled(mixed), untiled(grad_tokens), weight_grads


def solution(mesh):
    placed = (
        P("mp", None, "frame", None),
        P("mp", None, "frame", None),
        P(None, "frame", None),
        P(None, "frame", None),
        P(None, "frame", None),
        P(None, None, "mp"),
    )
    return jax.shard_map(
        on_device,
        mesh=mesh,
        in_specs=placed,
        out_specs=(
            P("mp", None, "frame", None),
            P("mp", None, "frame", None),
            P("frame", None, "mp"),
        ),
        check_vma=False,
    )
```

```python
from types import SimpleNamespace

import jax
import jax.numpy as jnp
from jax import lax
from jax.experimental import pallas as pl
from jax.experimental.pallas import tpu as pltpu
from jax.sharding import PartitionSpec as P

HD = 128
D = 3072
EPSILON = 1e-06
MESH = pl.DeviceIdType.MESH
BF16 = jnp.bfloat16
F32 = jnp.float32
MIB = 1024 * 1024
SPLIT = 2432


def dot(a, b, dims=((1,), (0,))):
    return lax.dot_general(a, b, (dims, ((), ())), preferred_element_type=F32)


NT = ((1,), (1,))
TN = ((0,), (0,))


class Ring:
    def __init__(self, index, device, stride):
        self.index, self.device, self.stride = index, device, stride

    def at(self, step):
        return lax.rem(self.index + (step + 4), 4)

    def to(self, step):
        return self.device(self.at(step))


class Links:
    def __init__(self, send_sems, recv_sems):
        self.send_sems, self.recv_sems = send_sems, recv_sems
        self.groups, self.sends = 0, []

    def send_group(self, whole):
        self.sends.append(whole)
        return len(self.sends) - 1

    def recv_group(self):
        self.groups += 1
        return self.groups - 1

    def copy(self, source, target, device, send, recv):
        return pltpu.make_async_remote_copy(
            src_ref=source,
            dst_ref=target,
            send_sem=self.send_sems.at[send],
            recv_sem=self.recv_sems.at[recv],
            device_id=device,
            device_id_type=MESH,
        )

    def wait(self, recv, whole):
        pltpu.make_async_copy(whole, whole, self.recv_sems.at[recv]).wait()

    def drain(self):
        for send, whole in enumerate(self.sends):
            pltpu.make_async_copy(whole, whole, self.send_sems.at[send]).wait()


def block_rows(first, second, one, two, half):
    block = first.at(one) * first.stride + second.at(two) * second.stride
    start = block * 32 + (0 if half is None else 16 * half)
    size = 32 if half is None else 16
    return pl.ds(pl.multiple_of(start, size), size)


def gather_steps(links, send, buffer, columns, first, second):
    class Group:
        def __init__(self, rows, *moves):
            self.whole, self.recv = buffer.at[0:rows, columns], links.recv_group()
            self.copies = []
            for ring, step, one, two, half in moves:
                part = buffer.at[block_rows(first, second, one, two, half), columns]
                self.copies.append(links.copy(part, part, ring.to(step), send, self.recv))

        def start(self):
            for made in self.copies:
                made.start()

        def wait(self):
            links.wait(self.recv, self.whole)

    places = (0, -1, 1, 2)
    ahead = Group(32, (first, 1, 0, 0, None))
    back = Group(32, (first, -1, 0, 0, None))
    across = Group(32, (first, 1, -1, 0, 0), (first, -1, 1, 0, 1))
    near = {one: Group(64, (second, 1, one, 0, None), (second, -1, one, 0, None)) for one in places}
    far = Group(
        128, *[move for one in places for move in ((second, 1, one, -1, 0), (second, -1, one, 1, 1))]
    )

    def begin():
        for group in (ahead, back, near[0]):
            group.start()

    def from_behind():
        ahead.wait()
        across.copies[0].start()
        near[-1].start()

    def from_ahead():
        back.wait()
        across.copies[1].start()
        near[1].start()

    def from_across():
        across.wait()
        near[2].start()

    def onward(place):
        def event():
            near[places[place]].wait()
            far.copies[2 * place].start()
            far.copies[2 * place + 1].start()

        return event

    return SimpleNamespace(
        begin=begin,
        behind=from_behind,
        ahead=from_ahead,
        across=from_across,
        on_own=onward(0),
        on_behind=onward(1),
        on_ahead=onward(2),
        on_across=onward(3),
        end=far.wait,
    )


def add_to(target, *others):
    total = target[...].astype(F32)
    for other in others:
        total = total + other[...].astype(F32)
    target[...] = total.astype(target.dtype)


class RingSum:
    def __init__(self, links, send, ring, piece, first, second):
        self.links, self.piece, self.first, self.second = links, piece, first, second
        ahead, back = ring.to(1), ring.to(-1)
        self.early, self.late = links.recv_group(), links.recv_group()

        def copy(source, target, device, recv):
            return links.copy(source, target, device, send, recv)

        self.far = (
            copy(piece(2, 0), first(0), ahead, self.early),
            copy(piece(2, 1), first(1), back, self.early),
        )
        self.own = (
            copy(piece(1, 1), second(0, 1), ahead, self.late),
            copy(piece(-1, 0), second(1, 0), back, self.late),
        )
        self.summed = (
            copy(piece(1, 0), second(0, 0), ahead, self.late),
            copy(piece(-1, 1), second(1, 1), back, self.late),
        )

    def begin_far(self):
        for made in self.far:
            made.start()

    def begin_own(self):
        for made in self.own:
            made.start()

    def onward(self):
        self.links.wait(self.early, self.first(None))
        for side, target in enumerate((self.piece(1, 0), self.piece(-1, 1))):
            add_to(target, self.first(side))
            self.summed[side].start()

    def end(self):
        self.links.wait(self.late, self.second(None, None))
        for half in range(2):
            add_to(self.piece(0, half), self.second(0, half), self.second(1, half))


def sides(land, *rest):
    def view(side, half=None):
        if side is None:
            return land.at[(slice(None), slice(None), *rest)]
        if half is None:
            return land.at[(side, slice(None), *rest)]
        size = land.shape[1] // 2
        return land.at[(side, slice(size * half, size * half + size), *rest)]

    return view


def scatter_steps(links, send, buffer, columns, first, second, land1, land2):
    def over_first(slot, two):
        return RingSum(
            links,
            send,
            first,
            lambda one, half: buffer.at[block_rows(first, second, one, two, half), columns],
            sides(land1.at[slot], columns),
            sides(land2.at[slot], columns),
        )

    rows = [over_first(slot, two) for slot, two in enumerate((2, -1, 1, 0))]
    column = RingSum(
        links,
        send,
        second,
        lambda two, half: buffer.at[block_rows(first, second, 0, two, half), columns],
        sides(land1.at[4], columns),
        sides(land2.at[4], columns),
    )

    return [*rows, column]


def softmax_rows(scores):
    shifted = jnp.exp(scores - jnp.max(scores, axis=-1, keepdims=True))
    return shifted / jnp.sum(shifted, axis=-1, keepdims=True)


def same_block():
    rows = lax.broadcasted_iota(jnp.int32, (HD, HD), 0)
    columns = lax.broadcasted_iota(jnp.int32, (HD, HD), 1)
    return (rows >> 5) == (columns >> 5)


def kernel(
    tokens_hbm, cotangent_hbm, shift_hbm, scale_hbm, gate_hbm, w_hbm, mixed, grad_tokens, dw,
    tokens, cotangent, shift, scale, gate, normed_in, scaled_in, branch_in, grad_in,
    land_normed, land_scaled, stage, units, inverses, parted, raw, stage_w,
    xall, w, qkv, grad_att, dall, turned, probs, branch, grad, dpart,
    land1b, land2b, land1g, land2g, land_core, land1y, land2y, land_z, flipped, core_out, core_in,
    send_sems, recv_sems, local_sems, out_sems, in_sems,
):
    f, m = lax.axis_index("frame"), lax.axis_index("mp")
    x, z = lax.rem(m, 4), lax.div(m, 4)
    core, y, zl = lax.rem(f, 2), lax.rem(lax.div(f, 2), 4), lax.div(f, 8)
    other = 1 - core
    ring_x = Ring(x, lambda to: (f, z * 4 + to), 1)
    ring_z = Ring(z, lambda to: (f, to * 4 + x), 4)
    ring_y = Ring(y, lambda to: (zl * 8 + to * 2 + core, m), 0)
    z_partner = ((1 - zl) * 8 + y * 2 + core, m)
    core_partner = (zl * 8 + y * 2 + other, m)
    links = Links(send_sems, recv_sems)

    own_rows = pl.ds(pl.multiple_of(m * 32, 32), 32)
    inputs = [
        pltpu.make_async_copy(source, target, local_sems.at[5 + number])
        for number, (source, target) in enumerate(
            (
                (tokens_hbm, tokens),
                (cotangent_hbm, cotangent),
                (shift_hbm, shift),
                (scale_hbm, scale),
                (gate_hbm, gate),
            )
        )
    ]
    for made in inputs:
        made.start()
    barrier = pltpu.get_barrier_semaphore()
    for ring in (ring_x, ring_z):
        for step in (1, -1):
            pl.semaphore_signal(barrier, inc=1, device_id=ring.to(step), device_id_type=MESH)

    @pl.loop(1, 16)
    def _(step):
        pl.semaphore_signal(
            barrier, inc=1, device_id=(lax.rem(f + step, 16), m), device_id_type=MESH
        )

    weigh = pltpu.make_async_copy(w_hbm, raw, local_sems.at[4])
    weigh.start()
    for made in inputs:
        made.wait()

    def total(values):
        eight = values[0:8]
        for tile in range(1, 6):
            eight = eight + values[8 * tile : 8 * tile + 8]
        eight = eight + pltpu.roll(eight, 2, 0)
        eight = eight + pltpu.roll(eight, 4, 0)
        eight = jnp.sum(eight, axis=-1, keepdims=True)
        return jnp.concatenate([eight] * 6, axis=0)

    def part_of(patch, clip):
        return pl.ds(pl.multiple_of((2 * patch + clip) * 48, 48), 48)

    def of_clip(clip):
        return slice(48 * clip, 48 * clip + 48)

    def unit_rows(rows):
        values = tokens[rows, :].astype(F32)
        inverse_rms = lax.rsqrt(total(values * values) * (1.0 / D) + EPSILON)
        return values * inverse_rms, jnp.broadcast_to(inverse_rms, values.shape)

    @pl.loop(0, 8)
    def _(patch):
        for clip in range(2):
            rows, own = part_of(patch, clip), of_clip(clip)
            unit, inverse_rms = unit_rows(rows)
            normed_in[rows, :] = (unit * (1.0 + scale[own, :]) + shift[own, :]).astype(BF16)
            units[rows, :], inverses[rows, :] = unit, inverse_rms

    def gate_cotangent():
        @pl.loop(0, 8)
        def _(patch):
            for clip in range(2):
                rows, own = part_of(patch, clip), of_clip(clip)
                scaled_in[rows, :] = (cotangent[rows, :].astype(F32) * gate[own, :]).astype(BF16)

    def mix():
        @pl.loop(0, 8)
        def _(patch):
            for clip in range(2):
                rows, own = part_of(patch, clip), of_clip(clip)
                mixed[rows, :] = (
                    tokens[rows, :].astype(F32) + gate[own, :] * branch_in[rows, :].astype(F32)
                ).astype(mixed.dtype)

    def grad_back():
        @pl.loop(0, 8)
        def _(patch):
            for clip in range(2):
                rows, own = part_of(patch, clip), of_clip(clip)
                unit, inverse_rms = units[rows, :], inverses[rows, :]
                grad_unit = grad_in[rows, :].astype(F32) * (1.0 + scale[own, :])
                correction = total(grad_unit * unit) * (1.0 / D)
                grad_tokens[rows, :] = (
                    cotangent[rows, :].astype(F32) + inverse_rms * (grad_unit - unit * correction)
                ).astype(grad_tokens.dtype)

    pl.semaphore_wait(barrier, 19)

    def exchange(number, source, target):
        def part(index):
            return pl.ds(pl.multiple_of(index * 48, 48), 48)

        def copy(step):
            to = lax.rem(f + step, 16)
            return pltpu.make_async_remote_copy(
                src_ref=source.at[part(to)],
                dst_ref=target.at[part(f)],
                send_sem=out_sems.at[number],
                recv_sem=in_sems.at[number],
                device_id=(to, m),
                device_id_type=MESH,
            )

        def here():
            return pltpu.make_async_copy(source.at[part(f)], target.at[part(f)], local_sems.at[number])

        def begin():
            @pl.loop(1, 16)
            def _(step):
                copy(step).start()

            here().start()

        def end():
            pltpu.make_async_copy(target.at[0:720], target.at[0:720], in_sems.at[number]).wait()
            here().wait()

        def sent():
            pltpu.make_async_copy(source.at[0:720], source.at[0:720], out_sems.at[number]).wait()

        sent_all.append(sent)
        return begin, end

    def assemble(landed, base):
        stage[...] = landed[...].astype(F32)
        for tile in range(24):
            for frame in range(2):
                xall[
                    pl.ds(pl.multiple_of(m * 32 + 16 * frame, 16), 16),
                    base + HD * tile : base + HD * tile + HD,
                ] = stage[pl.ds(2 * tile + frame, 16, stride=48), :].astype(BF16)

    def part_rows(buffer, number):
        for tile in range(24):
            for frame in range(2):
                stage[pl.ds(2 * tile + frame, 16, stride=48), :] = buffer[
                    pl.ds(pl.multiple_of(m * 32 + 16 * frame, 16), 16), HD * tile : HD * tile + HD
                ].astype(F32)
        parted[number] = stage[...].astype(BF16)

    sent_all = []
    normed_begin, normed_end = exchange(0, normed_in, land_normed)
    scaled_begin, scaled_end = exchange(1, scaled_in, land_scaled)
    branch_begin, branch_end = exchange(2, parted.at[0], branch_in)
    grad_begin, grad_end = exchange(3, parted.at[1], grad_in)

    def arrange(first, last):
        def event():
            @pl.loop(first, last)
            def _(part):
                stage_w[...] = raw[pl.ds(pl.multiple_of(part * 512, 512), 512), :].astype(F32)
                rows = pl.ds(pl.multiple_of(part * 64, 64), 64)
                for half in range(2):
                    for slot in range(4):
                        place = slot * 256 + half * HD
                        w[rows, place : place + HD] = stage_w[
                            pl.ds(4 * half + slot, 64, stride=8), :
                        ].astype(BF16)

        return event

    early, late = slice(0, SPLIT), slice(SPLIT, D)

    def gather(base):
        send = links.send_group(xall.at[0:480, base : base + D])
        return (
            gather_steps(links, send, xall, slice(base, base + SPLIT), ring_z, ring_x),
            gather_steps(links, send, xall, slice(base + SPLIT, base + D), ring_x, ring_z),
        )

    def scatter(buffer, *lands):
        send = links.send_group(buffer.at[0:480, :])
        return (
            scatter_steps(links, send, buffer, early, ring_x, ring_z, *lands),
            scatter_steps(links, send, buffer, late, ring_z, ring_x, *lands),
        )

    (na, nb), (sa, sb) = gather(0), gather(D)
    ba, bb = scatter(branch, land1b, land2b)
    ga, gb = scatter(grad, land1g, land2g)

    def chip_columns(y_to, zl_to):
        return pl.ds(pl.multiple_of(zl_to * 1536 + y_to * 384, 128), 384)

    mine = pl.multiple_of(core * 512, 512)
    theirs = pl.multiple_of(other * 512, 512)
    chunks = [(step, side) for side in (1, 0) for step in (2, 1, -1, 0)]
    core_copies, core_sends, first_core = {}, links.send_group(land_core), links.groups
    for step, side in chunks:
        columns = chip_columns(ring_y.at(step), lax.rem(zl + side, 2))
        core_copies[step, side] = links.copy(
            dpart.at[pl.ds(theirs, 512), columns], land_core.at[:, columns], core_partner,
            core_sends, links.recv_group(),
        )

    def over_y(side):
        zl_to = lax.rem(zl + side, 2)
        return RingSum(
            links,
            links.send_group(dpart.at[0:768, 0:768]),
            ring_y,
            lambda step, half: dpart.at[
                pl.ds(pl.multiple_of(mine + 256 * half, 256), 256), chip_columns(ring_y.at(step), zl_to)
            ],
            sides(land1y.at[side]),
            sides(land2y.at[side]),
        )

    y_sums = [over_y(0), over_y(1)]
    z_recv, core_recv = links.recv_group(), links.recv_group()
    z_copy = links.copy(
        dpart.at[pl.ds(mine, 512), chip_columns(y, 1 - zl)], land_z, z_partner,
        links.send_group(land_z), z_recv,
    )
    core_copy = links.copy(
        core_out, core_in, core_partner, links.send_group(core_in), core_recv
    )

    def project(slot):
        qkv[:, 256 * slot : 256 * slot + 256] = dot(
            xall[:, :D], w[:, 256 * slot : 256 * slot + 256]
        ).astype(BF16)

    def attend(group):
        def event():
            mask = same_block()
            rows = slice(group * HD, group * HD + HD)
            for head in range(2):
                query = qkv[rows, head * HD : head * HD + HD]
                key = qkv[rows, 256 + head * HD : 256 + head * HD + HD]
                value = qkv[rows, 512 + head * HD : 512 + head * HD + HD]
                scores = dot(query, key, NT) * (HD ** -0.5)
                attention = softmax_rows(jnp.where(mask, scores, -1e30))
                probs[group * 2 + head] = attention
                dall[rows, 768 + head * HD : 768 + head * HD + HD] = dot(
                    attention.astype(BF16), value
                ).astype(BF16)

        return event

    def branch_part(part):
        def event():
            @pl.loop(2 * part, 2 * part + 2)
            def _(step):
                rows = pl.ds(pl.multiple_of(step * 512, 512), 512)
                branch[:, rows] = dot(dall[:, 768:], w[rows, 768:], NT).astype(BF16)

        return event

    def back_project():
        grad_att[...] = dot(xall[:, D:], w[:, 768:]).astype(BF16)

    def attend_back(group):
        def event():
            rows = slice(group * HD, group * HD + HD)
            for head in range(2):
                low = slice(head * HD, head * HD + HD)
                query = qkv[rows, head * HD : head * HD + HD]
                key = qkv[rows, 256 + head * HD : 256 + head * HD + HD]
                value = qkv[rows, 512 + head * HD : 512 + head * HD + HD]
                incoming = grad_att[rows, low]
                attention = probs[group * 2 + head]
                grad_probs = dot(incoming, value, NT)
                inner = jnp.sum(grad_probs * attention, axis=-1, keepdims=True)
                grad_scores = (attention * (grad_probs - inner) * (HD ** -0.5)).astype(BF16)
                dall[rows, head * HD : head * HD + HD] = dot(grad_scores, key).astype(BF16)
                dall[rows, 256 + head * HD : 256 + head * HD + HD] = dot(
                    grad_scores, query, TN
                ).astype(BF16)
                dall[rows, 512 + head * HD : 512 + head * HD + HD] = dot(
                    attention.astype(BF16), incoming, TN
                ).astype(BF16)

        return event

    def grad_part(part):
        def event():
            @pl.loop(2 * part, 2 * part + 2)
            def _(step):
                rows = pl.ds(pl.multiple_of(step * 512, 512), 512)
                grad[:, rows] = dot(dall[:, :768], w[rows, :768], NT).astype(BF16)

        return event

    def turn():
        for part in range(8):
            turned[part * HD : part * HD + HD, :] = dall[:, part * HD : part * HD + HD].T

    def weight_chunk(step, side):
        def event():
            zl_to = lax.rem(zl + side, 2)
            columns = chip_columns(ring_y.at(step), zl_to)
            gated = pl.ds(pl.multiple_of(D + zl_to * 1536 + ring_y.at(step) * 384, 128), 384)
            dpart[:768, columns] = dot(turned[:768, :], xall[:, columns]).astype(BF16)
            dpart[768:, columns] = dot(turned[768:, :], xall[:, gated]).astype(BF16)
            core_copies[step, side].start()

        return event

    def core_sum(step, side):
        def event():
            columns = chip_columns(ring_y.at(step), lax.rem(zl + side, 2))
            links.wait(first_core + chunks.index((step, side)), land_core.at[:, columns])
            add_to(dpart.at[pl.ds(mine, 512), columns], land_core.at[:, columns])

        return event

    def z_end():
        links.wait(z_recv, land_z)
        columns = chip_columns(y, zl)
        total = dpart[pl.ds(mine, 512), columns].astype(F32) + land_z[...].astype(F32)
        flipped[...] = total.T
        core_out[...] = flipped[pl.ds(pl.multiple_of(other * 192, 192), 192), :].astype(BF16)
        core_copy.start()
        give(2 * core, flipped[pl.ds(pl.multiple_of(core * 192, 192), 192), :])

    def give(slot, values):
        for number in range(4):
            place = pl.ds(4 * (number % 2) + slot + number // 2, 192, stride=8)
            dw[place, :] = values[:, number * HD : number * HD + HD]

    def core_end():
        links.wait(core_recv, core_in)
        give(2 * other, core_in[...].astype(F32))

    def y_begin(side):
        def event():
            y_sums[side].begin_far()
            y_sums[side].begin_own()

        return event

    def in_turn(*steps):
        def event():
            for step in steps:
                step()

        return event

    take_scaled = in_turn(scaled_end, lambda: assemble(land_scaled, D))
    ar = [arrange(8 * part, 8 * part + 8) for part in range(6)]
    ar[0] = in_turn(weigh.wait, ar[0])
    pr = [lambda slot=slot: project(slot) for slot in range(3)]
    br, gr = ([make(part) for part in range(3)] for make in (branch_part, grad_part))
    at, ab = ([make(part) for part in range(4)] for make in (attend, attend_back))
    wc, cs = ([make(*chunk) for chunk in chunks] for make in (weight_chunk, core_sum))
    y_start = [y_begin(side) for side in range(2)]
    y_on = [each.onward for each in y_sums]
    y_end = [y_sums[0].end, in_turn(y_sums[1].end, z_copy.start)]
    give_branch = in_turn(lambda: part_rows(branch, 0), branch_begin)
    give_grad = in_turn(lambda: part_rows(grad, 1), grad_begin)
    take_branch, take_grad = in_turn(branch_end, mix), in_turn(grad_end, grad_back)

    plan = [
        na.begin, nb.begin, ar[0], ar[1], ar[2], ar[3], ar[4], ar[5], take_scaled, sa.begin, na.on_own,
        nb.behind, nb.ahead, sb.begin, na.ahead, na.behind, sa.on_own, nb.on_own, nb.across, sb.behind,
        sb.ahead, na.on_ahead, sa.behind, sa.ahead, nb.on_behind, na.on_behind, nb.on_ahead, sb.across,
        sb.on_own, na.across, sa.on_behind, nb.on_across, sa.on_ahead, sb.on_behind, sb.on_ahead,
        na.on_across, sa.across, sb.on_across, na.end, nb.end, pr[0], pr[1], pr[2], sa.on_across, at[0],
        at[1], at[2], at[3], br[0], br[1], br[2], ba[1].begin_own, bb[3].begin_own, ba[0].begin_far,
        bb[0].begin_far, ba[2].begin_own, bb[2].begin_far, ba[1].begin_far, ba[0].begin_own, bb[1].begin_far,
        bb[3].begin_far, ba[2].begin_far, bb[2].begin_own, bb[1].begin_own, sb.end, bb[0].begin_own, sa.end,
        back_project, ab[0], ab[1], ab[2], ab[3], gr[0], gr[1], gr[2], gb[3].begin_far, gb[2].begin_own,
        gb[1].begin_far, gb[3].begin_own, gb[2].begin_far, ga[0].begin_far, gb[0].begin_far, gb[1].begin_own,
        turn, wc[0], wc[1], wc[2], ba[0].onward, bb[0].onward, bb[3].onward, ga[0].begin_own, wc[3], wc[4],
        wc[5], ba[2].onward, cs[0], gb[0].begin_own, wc[6], wc[7], cs[1], ga[0].onward, cs[2], gb[1].onward,
        cs[3], y_start[1], ga[2].begin_far, gb[2].onward, cs[4], ba[1].onward, bb[2].onward, cs[5],
        gb[3].onward, ga[1].begin_far, cs[6], ba[0].end, ba[4].begin_far, gb[0].onward, cs[7], y_start[0],
        ga[2].begin_own, bb[0].end, ga[1].begin_own, bb[4].begin_far, bb[1].onward, bb[3].end, ba[2].end,
        gb[1].end, ga[0].end, ga[4].begin_far, gb[2].end, gb[4].begin_own, y_on[1], bb[2].end, ga[2].onward,
        gb[3].end, ba[1].end, ba[4].begin_own, ga[1].onward, ba[4].onward, gb[0].end, gb[4].begin_far,
        bb[1].end, bb[4].begin_own, ba[3].begin_own, bb[4].onward, ga[3].begin_far, y_on[0], ga[3].begin_own,
        ga[2].end, ga[1].end, ga[4].onward, ga[4].begin_own, gb[4].onward, ba[3].begin_far, bb[4].end,
        ga[3].onward, y_end[1], gb[4].end, ba[3].onward, y_end[0], ga[3].end, ga[4].end, give_grad,
        ba[3].end, ba[4].end, give_branch, z_end, take_grad, core_end, take_branch,
    ]
    normed_begin()
    gate_cotangent()
    scaled_begin()
    normed_end()
    assemble(land_normed, 0)
    for step in plan:
        step()
    links.drain()
    for sent in sent_all:
        sent()


def attention_block(tokens, cotangent, shift, scale, gate, weights):
    return pl.pallas_call(
        kernel,
        out_shape=(
            jax.ShapeDtypeStruct((768, HD), BF16),
            jax.ShapeDtypeStruct((768, HD), BF16),
            jax.ShapeDtypeStruct((1536, HD), F32),
        ),
        in_specs=[pl.BlockSpec(memory_space=pl.ANY)] * 6,
        out_specs=[pl.BlockSpec(memory_space=pltpu.VMEM)] * 3,
        scratch_shapes=[
            pltpu.VMEM((768, HD), BF16),
            pltpu.VMEM((768, HD), BF16),
            pltpu.VMEM((96, HD), F32),
            pltpu.VMEM((96, HD), F32),
            pltpu.VMEM((96, HD), F32),
            pltpu.VMEM((768, HD), BF16),
            pltpu.VMEM((768, HD), BF16),
            pltpu.VMEM((768, HD), BF16),
            pltpu.VMEM((768, HD), BF16),
            pltpu.VMEM((768, HD), BF16),
            pltpu.VMEM((768, HD), BF16),
            pltpu.VMEM((768, HD), F32),
            pltpu.VMEM((768, HD), F32),
            pltpu.VMEM((768, HD), F32),
            pltpu.VMEM((2, 768, HD), BF16),
            pltpu.VMEM((24576, HD), BF16),
            pltpu.VMEM((512, HD), F32),
            pltpu.VMEM((512, 2 * D), BF16),
            pltpu.VMEM((D, 1024), BF16),
            pltpu.VMEM((512, 768), BF16),
            pltpu.VMEM((512, 256), BF16),
            pltpu.VMEM((512, 1024), BF16),
            pltpu.VMEM((1024, 512), BF16),
            pltpu.VMEM((8, HD, HD), F32),
            pltpu.VMEM((512, D), BF16),
            pltpu.VMEM((512, D), BF16),
            pltpu.VMEM((1024, D), BF16),
            pltpu.VMEM((5, 2, 16, D), BF16),
            pltpu.VMEM((5, 2, 32, D), BF16),
            pltpu.VMEM((5, 2, 16, D), BF16),
            pltpu.VMEM((5, 2, 32, D), BF16),
            pltpu.VMEM((512, D), BF16),
            pltpu.VMEM((2, 2, 256, 384), BF16),
            pltpu.VMEM((2, 2, 512, 384), BF16),
            pltpu.VMEM((512, 384), BF16),
            pltpu.VMEM((384, 512), F32),
            pltpu.VMEM((192, 512), BF16),
            pltpu.VMEM((192, 512), BF16),
            pltpu.SemaphoreType.DMA((9,)),
            pltpu.SemaphoreType.DMA((86,)),
            pltpu.SemaphoreType.DMA((10,)),
            pltpu.SemaphoreType.DMA((4,)),
            pltpu.SemaphoreType.DMA((4,)),
        ],
        compiler_params=pltpu.CompilerParams(
            collective_id=0, has_side_effects=True, vmem_limit_bytes=60 * MIB
        ),
    )(tokens, cotangent, shift, scale, gate, weights)


def copy_kernel(*refs):
    half = len(refs) // 2
    for source, target in zip(refs[:half], refs[half:]):
        target[...] = source[...]


def copied(*arrays):
    return pl.pallas_call(
        copy_kernel,
        out_shape=[jax.ShapeDtypeStruct(each.shape, each.dtype) for each in arrays],
        in_specs=[pl.BlockSpec(memory_space=pltpu.VMEM)] * len(arrays),
        out_specs=[pl.BlockSpec(memory_space=pltpu.VMEM)] * len(arrays),
    )(*arrays)


def on_device(tokens, cotangent, mod_shift, mod_scale, mod_gate, attn_weights):
    weights = attn_weights.reshape(D, 4, 2, HD).transpose(0, 2, 1, 3).reshape(8 * D, HD)
    def tiles(values):
        lead = values.shape[:-2]
        return jnp.swapaxes(values.reshape(*lead, 2, 24, HD), -2, -3).reshape(-1, HD)

    def untiled(values):
        return jnp.swapaxes(values.reshape(8, 2, 24, 2, HD), -2, -3).reshape(8, 2, 2, D)

    mixed, grad_tokens, weight_grads = attention_block(
        tiles(tokens), tiles(cotangent), tiles(mod_shift), tiles(mod_scale), tiles(mod_gate), weights
    )
    mixed, grad_tokens, weight_grads = copied(mixed, grad_tokens, weight_grads)
    weight_grads = weight_grads.reshape(192, 2, 4, HD).transpose(0, 2, 1, 3).reshape(192, 4, 256)
    return untiled(mixed), untiled(grad_tokens), weight_grads


def solution(mesh):
    placed = (
        P("mp", None, "frame", None),
        P("mp", None, "frame", None),
        P(None, "frame", None),
        P(None, "frame", None),
        P(None, "frame", None),
        P(None, None, "mp"),
    )
    return jax.shard_map(
        on_device,
        mesh=mesh,
        in_specs=placed,
        out_specs=(
            P("mp", None, "frame", None),
            P("mp", None, "frame", None),
            P("frame", None, "mp"),
        ),
        check_vma=False,
    )
```
